32 devices in a mesh: mem: 8 (over y, x, core), tile: 4 (over z).
Axes of the slice: x: 2, y: 2, z: 4, core: 2. Of those that a mesh axis runs over, the one named last changes fastest.
Arguments:
- latents: bfloat16 [16, 16, 8192], P('mem', 'tile'), may hold values from -3 to 3
- in_weight: bfloat16 [2, 576, 256], replicated, may hold values from -0.25 to 0.25
- out_weight: bfloat16 [2, 2304, 64], replicated, may hold values from -0.125 to 0.125
- observe_weight: bfloat16 [576, 8], replicated, may hold values from -0.25 to 0.25
- obs_cells: int32 [16, 32], P('tile'), may hold values from 0 to 127, all different within a row
- obs_values: float32 [16, 256], P('tile'), may hold values from -6 to 6
- obs_precision: float32 [16, 256], P('tile'), may hold values from 0.3 to 3
Outputs:
- analysis: float32 [16, 16, 8192], P('mem', 'tile')
- covariance: float32 [16, 16], replicated
The draws below stay inside these ranges and needn't reach their ends.
Inputs may be any that keep to these rules, and one draw needn't show every extreme that they name: `obs_cells`: each row lists 32 different columns of the slab.
All inputs are finite; a program needn't handle non-finite values.
Results may differ from the reference program's by a relative error of at most 0.009.
Values may be sent and summed in bfloat16 or wider, within the bound.
A program may use at most 64 MiB of HBM per device.

```python
import math
import jax
import jax.numpy as jnp
from jax import lax

MEM_DEV = 2
COLS = 128
CH = 64
HID = 256
OBS_COLS = 32
OBS_CH = 8
ENS = 16
ROWS = 16


def block_levels(rng, shape, cuts, smallest, top_value):
    factor_of, own = 1.0, jax.random.fold_in(rng, 6)
    for axis_at, blocks in cuts:
        draws = jnp.exp(jax.random.uniform(jax.random.fold_in(own, axis_at), (blocks,), jnp.float32, smallest / len(cuts), top_value / len(cuts)))
        factor_of = factor_of * jnp.repeat(draws, shape[axis_at] // blocks).reshape([-1 if axis == axis_at else 1 for axis in range(len(shape))])
    return factor_of


def distinct(rng, rows, count, top, lift):
    order = jax.random.permutation(jax.random.fold_in(rng, 1), count)
    favour = order
    for power in range(3):
        favour = favour * favour // count
    favour = favour * lift // count
    chance = jax.random.randint(jax.random.fold_in(rng, 2), (rows, count), 0, 4096) + favour
    sure = jax.random.permutation(jax.random.fold_in(rng, 3), rows)[jnp.arange(count) % rows]
    chance = jnp.where(jnp.arange(rows)[:, None] == sure[None, :], 1 << 14, chance)
    score = chance * count + jnp.arange(count)
    return lax.top_k(score.astype(jnp.int32), top)[1].astype(jnp.int32)


def gaussian(key, dims, width, reach, split=(), kind=jnp.bfloat16):
    array = jax.random.normal(key, dims, jnp.float32) * width
    if len(split) > 0:
        array = block_levels(key, dims, split, -0.22, 0.18) * array
    return jnp.clip(array, min=-reach, max=reach).astype(kind)


def setup_inputs(seed: int = 0) -> dict:
    splits = jax.random.split(jax.random.key(seed), 8)
    latents = gaussian(splits[0], (ENS, ROWS, COLS * CH), 0.5, 3.0, ((0, 8), (1, 4)))
    in_weight = gaussian(splits[1], (2, 9 * CH, HID), (9 * CH) ** -0.5, 0.25)
    out_weight = gaussian(splits[2], (2, 9 * HID, CH), (9 * HID) ** -0.5, 0.125)
    observe_weight = gaussian(splits[3], (9 * CH, OBS_CH), (9 * CH) ** -0.5, 0.25)
    obs_cells = distinct(splits[4], ROWS, COLS, OBS_COLS, 0)
    obs_values = gaussian(splits[5], (ROWS, OBS_COLS * OBS_CH), 1.0, 6.0, ((0, 4),), jnp.float32)
    obs_precision = jnp.clip(jnp.exp(math.log(3.0) - 2.3025851 * jax.random.uniform(splits[6], (ROWS, OBS_COLS * OBS_CH), jnp.float32) ** block_levels(splits[6], (ROWS, OBS_COLS * OBS_CH), ((0, 4),), -0.2, 0.2)), 0.3, 3.0)
    return {"latents": latents, "in_weight": in_weight, "out_weight": out_weight, "observe_weight": observe_weight, "obs_cells": obs_cells, "obs_values": obs_values, "obs_precision": obs_precision}


eps = 1e-06
guide_step = 0.5

def rms_norm(values):
    return values * lax.rsqrt(lax.optimization_barrier(jnp.mean(values * values, axis=-1, keepdims=True)) + eps)

def pad_all(values):
    return jnp.pad(values, ((0, 0), (1, 1), (1, 1), (0, 0)))

def conv_rows(padded, weight):
    row_count = padded.shape[1] - 2
    col_count = padded.shape[2] - 2
    in_ch = padded.shape[3]
    summed = None
    for row_tap in range(3):
        row_band = padded[:, row_tap:row_tap + row_count]
        col_patch = jnp.concatenate([row_band[:, :, col_tap:col_tap + col_count] for col_tap in range(3)], axis=-1)
        part_sum = jnp.dot(col_patch, weight[row_tap * 3 * in_ch:(row_tap + 1) * 3 * in_ch], preferred_element_type=jnp.float32)
        summed = part_sum if summed is None else summed + part_sum
    return summed

def res_block(current, first_weight, second_weight):
    normed = rms_norm(current.astype(jnp.float32)).astype(jnp.bfloat16)
    hidden = jax.nn.silu(conv_rows(pad_all(normed), first_weight)).astype(jnp.bfloat16)
    return (current.astype(jnp.float32) + conv_rows(pad_all(hidden), second_weight)).astype(jnp.bfloat16)

def observe_padded(padded, obs_cells, observe_weight):
    row_count = padded.shape[1] - 2
    patches = []
    for row_tap in range(3):
        row_band = padded[:, row_tap:row_tap + row_count]
        for col_tap in range(3):
            col_index = (obs_cells + col_tap)[None, :, :, None]
            patches.append(jnp.take_along_axis(row_band, col_index, axis=2))
    stacked = jnp.concatenate(patches, axis=-1)
    predicted = jnp.dot(stacked, observe_weight, preferred_element_type=jnp.float32)
    return predicted.reshape(predicted.shape[0], predicted.shape[1], -1)

def reference(latents, in_weight, out_weight, observe_weight, obs_cells, obs_values, obs_precision):
    blocks = latents.reshape(ENS // MEM_DEV, MEM_DEV, ROWS, COLS, CH)

    def denoise(member_block):
        current = member_block
        for layer_idx in range(2):
            current = res_block(current, in_weight[layer_idx], out_weight[layer_idx])
        return (current, observe_padded(pad_all(current), obs_cells, observe_weight))
    denoised, predicted = lax.map(denoise, blocks)
    denoised = denoised.reshape(ENS, ROWS, COLS * CH)
    predicted = predicted.reshape(ENS, ROWS, OBS_COLS * OBS_CH)
    ens_mean = lax.optimization_barrier(jnp.mean(predicted, axis=0))
    anomaly = predicted - ens_mean
    innovation = obs_values - predicted
    covariance = jnp.einsum('jrc,mrc->jm', anomaly * obs_precision, innovation, precision=lax.Precision.HIGHEST)
    covariance = covariance / (ROWS * OBS_COLS * OBS_CH)

    def update_row(row_state):
        values = row_state.astype(jnp.float32)
        spread = values - lax.optimization_barrier(jnp.mean(values, axis=0))
        moved = jnp.einsum('jc,jm->mc', spread, covariance, precision=lax.Precision.HIGHEST)
        return values + guide_step * moved
    analysis = jnp.transpose(lax.map(update_row, jnp.transpose(denoised, (1, 0, 2))), (1, 0, 2))
    return (analysis, covariance)
```

```python
import functools

import jax
import jax.numpy as jnp
from jax import lax
from jax.experimental import pallas as pl
from jax.experimental.pallas import tpu as pltpu
from jax.sharding import PartitionSpec as P

EPS = 1e-06
GUIDE_STEP = 0.5
HALO = 4
BF16 = jnp.bfloat16
F32 = jnp.float32
HIGHEST = lax.Precision.HIGHEST


def iota(shape, axis):
    return lax.broadcasted_iota(jnp.int32, shape, axis)


def neighbours(values, pairs, half, swap):
    count = values.shape[0]
    pair = iota(values.shape, 0) % pairs
    lane = iota(values.shape, 1)
    following = jnp.where(pair == pairs - 1, 0.0, pltpu.roll(values, count - 1, 0))
    previous = jnp.where(pair == 0, 0.0, pltpu.roll(values, 1, 0))
    if swap:
        following, previous = previous, following
    return jnp.where(lane < half, following, previous)


def kernel(
    sizes, lat, w_in, w_out, w_obs, cells, values, precision, out, cov_out,
    raw, frame, hid, cur, big_in, big_out, big_obs, patch, gathered, edge, preds, covs,
    halo_send, halo_recv, edge_send, edge_recv, pred_send, pred_recv,
    bulk_send, fwd_send, bulk_recv, cov_send, cov_recv,
):
    mem_n, tile_n = sizes
    members, rows, pairs, lanes = lat.shape
    half = lanes // 2
    hidden = w_in.shape[2]
    obs_cols = cells.shape[1]
    obs_lanes = values.shape[1]
    obs_ch = w_obs.shape[1]
    ens = mem_n * members
    me, tile = lax.axis_index("mem"), lax.axis_index("tile")
    ext = rows + 2 * HALO

    def mem_peer(k):
        return lax.rem(me + k, mem_n)

    def tile_peer(k):
        return lax.rem(tile + k, tile_n)

    barrier = pltpu.get_barrier_semaphore()
    for k in range(1, mem_n):
        pl.semaphore_signal(barrier, inc=1, device_id={"mem": mem_peer(k)}, device_id_type=pl.DeviceIdType.MESH)
    for k in range(1, tile_n):
        pl.semaphore_signal(barrier, inc=1, device_id={"tile": tile_peer(k)}, device_id_type=pl.DeviceIdType.MESH)
    pl.semaphore_wait(barrier, mem_n - 1 + tile_n - 1)

    def remote(src, dst, send, recv, axis, index):
        return pltpu.make_async_remote_copy(
            src_ref=src, dst_ref=dst, send_sem=send, recv_sem=recv,
            device_id={axis: index}, device_id_type=pl.DeviceIdType.MESH,
        )

    to_next = remote(
        lat.at[:, pl.ds(rows - HALO, HALO)], raw.at[:, pl.ds(0, HALO)],
        halo_send.at[0], halo_recv.at[0], "tile", jnp.minimum(tile + 1, tile_n - 1),
    )
    to_prev = remote(
        lat.at[:, pl.ds(0, HALO)], raw.at[:, pl.ds(HALO + rows, HALO)],
        halo_send.at[1], halo_recv.at[1], "tile", jnp.maximum(tile - 1, 0),
    )
    has_next, has_prev = tile < tile_n - 1, tile > 0
    pl.when(has_next)(lambda: to_next.start())
    pl.when(has_prev)(lambda: to_prev.start())

    def pair_weight(dest, layer, source, width, base, even_at, odd_at):
        ch = half
        zero = jnp.zeros((ch, width), BF16)
        for di in range(3):
            tap = lambda dj: source(di, dj)
            top = base + di * 4 * ch
            blocks = ((tap(1), tap(0)), (tap(2), tap(1)), (zero, tap(2)), (tap(0), zero))
            for b, (even, odd) in enumerate(blocks):
                er, ec = even_at
                orow, oc = odd_at
                dest[layer, pl.ds(er + top + b * ch, ch), pl.ds(ec, width)] = even
                dest[layer, pl.ds(orow + top + b * ch, ch), pl.ds(oc, width)] = odd

    def build_in(layer):
        pair_weight(
            big_in, layer, lambda di, dj: w_in[layer, pl.ds((di * 3 + dj) * half, half), :],
            hidden, 0, (0, 0), (0, hidden),
        )

    def build_out(layer):
        zero = jnp.zeros((hidden, half), BF16)
        for di in range(3):
            tap = lambda dj: w_out[layer, pl.ds((di * 3 + dj) * hidden, hidden), :]
            t0, t1, t2 = tap(0), tap(1), tap(2)
            top = di * 2 * hidden
            big_out[layer, pl.ds(top, hidden), pl.ds(0, lanes)] = jnp.concatenate([t1, t0], axis=1)
            big_out[layer, pl.ds(top, hidden), pl.ds(lanes, lanes)] = jnp.concatenate([zero, t2], axis=1)
            big_out[layer, pl.ds(top + hidden, hidden), pl.ds(0, lanes)] = jnp.concatenate([t2, t1], axis=1)
            big_out[layer, pl.ds(top + hidden, hidden), pl.ds(lanes, lanes)] = jnp.concatenate([t0, zero], axis=1)

    ones = (iota((2 * lanes, lanes), 0) // half % 2 == iota((2 * lanes, lanes), 1) // half).astype(BF16)

    def norm_frame(x):
        wide = x.astype(F32)
        square = wide * wide
        high = square.astype(BF16)
        low = (square - high.astype(F32)).astype(BF16)
        total = jnp.dot(jnp.concatenate([high, low], axis=1), ones, preferred_element_type=F32)
        normed = wide * lax.rsqrt(total * (1.0 / half) + EPS)
        return with_sides(normed)

    def with_sides(v):
        return jnp.concatenate([v, neighbours(v, pairs, half, False)], axis=1).astype(BF16)

    def flat(ref, m, start, count):
        return ref[m, pl.ds(start, count)].reshape(count * pairs, ref.shape[-1])

    def put(ref, m, start, count, value):
        ref[m, pl.ds(start, count)] = value.reshape(count, pairs, ref.shape[-1])

    def taps(ref, m, start, count):
        return jnp.concatenate([flat(ref, m, start + d - 1, count) for d in range(3)], axis=1)

    def conv_in(layer, m, start, count):
        summed = jnp.dot(taps(frame, m, start, count), big_in[layer], preferred_element_type=F32)
        act = 0.5 * summed * (1.0 + jnp.tanh(0.5 * summed))
        put(hid, m, start, count, act.astype(BF16))

    def conv_out(layer, m, start, count, before):
        summed = jnp.dot(taps(hid, m, start, count), big_out[layer], preferred_element_type=F32)
        summed = summed[:, :lanes] + neighbours(summed[:, lanes:], pairs, half, True)
        return (before.astype(F32) + summed).astype(BF16)

    def blank(ref, low, high):
        def clear(start, count):
            ref[:, pl.ds(start, count)] = jnp.zeros((members, count) + ref.shape[2:], BF16)
        pl.when(tile == 0)(lambda: clear(low, HALO - low))
        pl.when(tile == tile_n - 1)(lambda: clear(HALO + rows, high - HALO - rows))

    build_in(0)
    for m in range(members):
        put(frame, m, HALO, rows, norm_frame(lat[m].reshape(rows * pairs, lanes)))
    for m in range(members):
        conv_in(0, m, HALO + 1, rows - 2)
    build_out(0)
    build_in(1)
    build_out(1)
    spread_lanes = (iota((obs_ch, obs_lanes), 1) % obs_ch == iota((obs_ch, obs_lanes), 0)).astype(BF16)
    tiled = jnp.dot(w_obs[...], spread_lanes, preferred_element_type=F32).astype(BF16)
    pair_weight(
        big_obs, 0, lambda di, dj: tiled[(di * 3 + dj) * half : (di * 3 + dj + 1) * half],
        obs_lanes, 0, (0, 0), (12 * half, 0),
    )
    eye = (iota((obs_cols, obs_cols), 0) == iota((obs_cols, obs_cols), 1)).astype(BF16)
    cells_t = lax.dot_general(
        eye, cells[...].astype(F32).astype(BF16), (((1,), (1,)), ((), ())), preferred_element_type=F32
    ).astype(jnp.int32)

    pl.when(has_prev)(lambda: to_next.wait_recv())
    pl.when(has_next)(lambda: to_prev.wait_recv())
    blank(raw, 0, ext)
    for m in range(members):
        put(frame, m, 0, HALO, norm_frame(flat(raw, m, 0, HALO)))
        put(frame, m, HALO + rows, HALO, norm_frame(flat(raw, m, HALO + rows, HALO)))
        conv_in(0, m, 1, HALO)
        conv_in(0, m, HALO + rows - 1, HALO)
    blank(hid, 1, ext - 1)
    for m in range(members):
        before = jnp.concatenate([
            flat(raw, m, 2, HALO - 2), lat[m].reshape(rows * pairs, lanes), flat(raw, m, HALO + rows, HALO - 2)
        ], axis=0)
        put(cur, m, 2, ext - 4, conv_out(0, m, 2, ext - 4, before))
    blank(cur, 2, ext - 2)
    for m in range(members):
        put(frame, m, 2, ext - 4, norm_frame(flat(cur, m, 2, ext - 4)))
        conv_in(1, m, 3, ext - 6)
    blank(hid, 3, ext - 3)
    for m in range(members):
        done = conv_out(1, m, HALO, rows, flat(cur, m, HALO, rows))
        gathered[me, m] = done.reshape(rows, pairs, lanes)

    edge_next = remote(
        gathered.at[me, :, rows - 1], edge.at[0], edge_send.at[0], edge_recv.at[0],
        "tile", jnp.minimum(tile + 1, tile_n - 1),
    )
    edge_prev = remote(
        gathered.at[me, :, 0], edge.at[1], edge_send.at[1], edge_recv.at[1],
        "tile", jnp.maximum(tile - 1, 0),
    )
    pl.when(has_next)(lambda: edge_next.start())
    pl.when(has_prev)(lambda: edge_prev.start())

    step = 2 if mem_n % 2 == 0 else 1
    sibling = me + 1 - 2 * lax.rem(me, 2)
    bulk = []
    for k in range(step, mem_n, step):
        bulk.append(remote(
            gathered.at[me], gathered.at[me], bulk_send.at[k], bulk_recv.at[me], "mem", mem_peer(k)
        ))
    if step == 2:
        bulk.append(remote(
            gathered.at[me], gathered.at[me], bulk_send.at[0], bulk_recv.at[me], "mem", sibling
        ))
    for copy in bulk:
        copy.start()

    for m in range(members):
        put(frame, m, HALO, rows, with_sides(gathered[me, m].astype(F32).reshape(rows * pairs, lanes)))
    pl.when(has_prev)(lambda: edge_next.wait_recv())
    pl.when(has_next)(lambda: edge_prev.wait_recv())

    @pl.when(tile == 0)
    def _():
        edge[0] = jnp.zeros(edge.shape[1:], BF16)

    @pl.when(tile == tile_n - 1)
    def _():
        edge[1] = jnp.zeros(edge.shape[1:], BF16)

    for m in range(members):
        frame[m, HALO - 1] = with_sides(edge[0, m].astype(F32))
        frame[m, HALO + rows] = with_sides(edge[1, m].astype(F32))
    column = 2 * iota((obs_cols, pairs), 1)
    for r in range(rows):
        here = cells_t[:, r : r + 1]
        pick = jnp.concatenate([(here == column), (here == column + 1)], axis=0).astype(BF16)
        around = jnp.concatenate([taps(frame, m, HALO + r, 1) for m in range(members)], axis=1)
        got = jnp.dot(pick, around, preferred_element_type=F32).astype(BF16)
        wide = 12 * half
        for m in range(members):
            part = got[:, m * wide : (m + 1) * wide]
            at = pl.ds((m * rows + r) * obs_cols, obs_cols)
            patch[at, pl.ds(0, wide)] = part[:obs_cols]
            patch[at, pl.ds(wide, wide)] = part[obs_cols:]
    spread_pred = jnp.dot(patch[...], big_obs[0], preferred_element_type=F32)
    spread_pred = spread_pred.reshape(members * rows, obs_cols, obs_lanes)
    own = iota(spread_pred.shape, 1) == iota(spread_pred.shape, 2) // obs_ch
    preds[me] = jnp.sum(jnp.where(own, spread_pred, 0.0), axis=1)

    pred_copies = [
        remote(preds.at[me], preds.at[me], pred_send.at[k], pred_recv.at[me], "mem", mem_peer(k))
        for k in range(1, mem_n)
    ]
    for copy in pred_copies:
        copy.start()
    for k in range(1, mem_n):
        j = mem_peer(k)
        remote(preds.at[j], preds.at[j], pred_send.at[k], pred_recv.at[j], "mem", j).wait_recv()

    per = members * rows
    everyone = preds[...]
    total = jnp.sum(everyone, axis=0)
    mean = total[:rows]
    for m in range(1, members):
        mean = mean + total[m * rows : (m + 1) * rows]
    mean = jnp.concatenate([mean * (1.0 / ens)] * members, axis=0)
    weight = jnp.concatenate([precision[...]] * members, axis=0)
    target = jnp.concatenate([values[...]] * members, axis=0)
    left = ((everyone - mean[None]) * weight[None]).reshape(mem_n * per, obs_lanes)
    right = (target[None] - everyone).reshape(mem_n * per, obs_lanes)
    gram = lax.dot_general(
        left, right, (((1,), (1,)), ((), ())), precision=HIGHEST, preferred_element_type=F32
    )
    side = mem_n * per
    same = iota((side, side), 0) % rows == iota((side, side), 1) % rows
    gram = jnp.where(same, gram, 0.0)
    fold = (iota((ens, side), 1) // rows == iota((ens, side), 0)).astype(F32)
    gram = jnp.dot(fold, gram, precision=HIGHEST, preferred_element_type=F32)
    part = lax.dot_general(
        gram, fold, (((1,), (1,)), ((), ())), precision=HIGHEST, preferred_element_type=F32
    )
    covs[tile] = jnp.concatenate([part, jnp.zeros((ens, covs.shape[2] - ens), F32)], axis=1)
    cov_copies = [
        remote(covs.at[tile], covs.at[tile], cov_send.at[k], cov_recv.at[tile], "tile", tile_peer(k))
        for k in range(1, tile_n)
    ]
    for copy in cov_copies:
        copy.start()

    forwards = []
    if step == 2:
        for k in range(2, mem_n, 2):
            j = mem_peer(k)
            remote(gathered.at[j], gathered.at[j], bulk_send.at[k], bulk_recv.at[j], "mem", j).wait_recv()
            copy = remote(gathered.at[j], gathered.at[j], fwd_send.at[k], bulk_recv.at[j], "mem", sibling)
            copy.start()
            forwards.append(copy)

    for k in range(1, tile_n):
        j = tile_peer(k)
        remote(covs.at[j], covs.at[j], cov_send.at[k], cov_recv.at[j], "tile", j).wait_recv()
    cov = covs[0]
    for j in range(1, tile_n):
        cov = cov + covs[j]
    cov = cov[:, :ens] * (1.0 / (rows * tile_n * obs_lanes))
    cov_out[...] = cov
    centred = GUIDE_STEP * (cov - jnp.mean(cov, axis=0, keepdims=True))
    factors = []
    for q in range(members):
        mine = iota((ens, ens), 1) == me * members + q
        column_q = jnp.sum(jnp.where(mine, centred, 0.0), axis=1, keepdims=True)
        factors.append(jnp.broadcast_to(column_q, (ens, lanes)))

    if step == 2:
        for k in range(1, mem_n, 2):
            j = mem_peer(k)
            remote(gathered.at[j], gathered.at[j], bulk_send.at[0], bulk_recv.at[j], "mem", j).wait_recv()
    else:
        for k in range(1, mem_n):
            j = mem_peer(k)
            remote(gathered.at[j], gathered.at[j], bulk_send.at[k], bulk_recv.at[j], "mem", j).wait_recv()
    for r in range(rows):
        acc = [gathered[me, q, r].astype(F32) for q in range(members)]
        for j in range(ens):
            value = gathered[j // members, j % members, r].astype(F32)
            for q in range(members):
                acc[q] = acc[q] + factors[q][j : j + 1] * value
        for q in range(members):
            out[q, r] = acc[q]

    pl.when(has_next)(lambda: to_next.wait_send())
    pl.when(has_prev)(lambda: to_prev.wait_send())
    pl.when(has_next)(lambda: edge_next.wait_send())
    pl.when(has_prev)(lambda: edge_prev.wait_send())
    for copy in bulk + pred_copies + cov_copies + forwards:
        copy.wait_send()


def per_device(sizes, latents, in_weight, out_weight, observe_weight, obs_cells, obs_values, obs_precision):
    mem_n, tile_n = sizes
    members, rows, flat_count = latents.shape
    half = observe_weight.shape[0] // 9
    lanes = 2 * half
    pairs = flat_count // lanes
    hidden = in_weight.shape[2]
    obs_cols, obs_lanes = obs_cells.shape[1], obs_values.shape[1]
    ens = mem_n * members
    ext = rows + 2 * HALO
    vmem = pl.BlockSpec(memory_space=pltpu.VMEM)
    dma = pltpu.SemaphoreType.DMA
    analysis, covariance = pl.pallas_call(
        functools.partial(kernel, sizes),
        out_shape=(
            jax.ShapeDtypeStruct((members, rows, pairs, lanes), F32),
            jax.ShapeDtypeStruct((ens, ens), F32),
        ),
        in_specs=[vmem] * 7,
        out_specs=(vmem, vmem),
        scratch_shapes=[
            pltpu.VMEM((members, ext, pairs, lanes), BF16),
            pltpu.VMEM((members, ext, pairs, 2 * lanes), BF16),
            pltpu.VMEM((members, ext, pairs, 2 * hidden), BF16),
            pltpu.VMEM((members, ext, pairs, lanes), BF16),
            pltpu.VMEM((2, 12 * half, 2 * hidden), BF16),
            pltpu.VMEM((2, 6 * hidden, 2 * lanes), BF16),
            pltpu.VMEM((1, 24 * half, obs_lanes), BF16),
            pltpu.VMEM((members * rows * obs_cols, 24 * half), BF16),
            pltpu.VMEM((mem_n, members, rows, pairs, lanes), BF16),
            pltpu.VMEM((2, members, pairs, lanes), BF16),
            pltpu.VMEM((mem_n, members * rows, obs_lanes), F32),
            pltpu.VMEM((tile_n, ens, 128), F32),
            dma((2,)), dma((2,)), dma((2,)), dma((2,)),
            dma((mem_n,)), dma((mem_n,)),
            dma((mem_n,)), dma((mem_n,)), dma((mem_n,)),
            dma((tile_n,)), dma((tile_n,)),
        ],
        compiler_params=pltpu.CompilerParams(
            collective_id=0, has_side_effects=True, vmem_limit_bytes=48 * 1024 * 1024
        ),
    )(
        latents.reshape(members, rows, pairs, lanes), in_weight, out_weight, observe_weight,
        obs_cells, obs_values, obs_precision,
    )
    return analysis.reshape(members, rows, flat_count), covariance


def solution(mesh):
    in_specs = (
        P("mem", "tile", None), P(), P(), P(), P("tile", None), P("tile", None), P("tile", None),
    )
    out_specs = (P("mem", "tile", None), P())
    sizes = (mesh.shape["mem"], mesh.shape["tile"])
    return jax.shard_map(
        functools.partial(per_device, sizes), mesh=mesh, in_specs=in_specs, out_specs=out_specs, check_vma=False
    )
```

```python
import functools

import jax
import jax.numpy as jnp
from jax import lax
from jax.experimental import pallas as pl
from jax.experimental.pallas import tpu as pltpu
from jax.sharding import PartitionSpec as P

EPS = 1e-06
GUIDE_STEP = 0.5
HALO = 4
BF16 = jnp.bfloat16
F32 = jnp.float32
HIGHEST = lax.Precision.HIGHEST


def iota(shape, axis):
    return lax.broadcasted_iota(jnp.int32, shape, axis)


def neighbours(values, pairs, half, swap):
    count = values.shape[0]
    pair = iota(values.shape, 0) % pairs
    lane = iota(values.shape, 1)
    following = jnp.where(pair == pairs - 1, 0.0, pltpu.roll(values, count - 1, 0))
    previous = jnp.where(pair == 0, 0.0, pltpu.roll(values, 1, 0))
    if swap:
        following, previous = previous, following
    return jnp.where(lane < half, following, previous)


def kernel(
    sizes, lat, w_in, w_out, w_obs, cells, values, precision, out, cov_out,
    halo, stage, raw, frame, hid, cur, big_in, big_out, big_obs, patch, gathered, edge, preds, chunks, covs,
    halo_send, halo_recv, edge_send, edge_recv, pred_send, pred_recv,
    bulk_send, fwd_send, bulk_recv, cov_send, cov_recv,
):
    mem_n, tile_n = sizes
    members, rows, flat_count = lat.shape
    half = w_obs.shape[1] // 9
    lanes = 2 * half
    pairs = flat_count // lanes
    hidden = w_in.shape[2]
    obs_cols = cells.shape[1]
    obs_lanes = values.shape[1]
    obs_ch = w_obs.shape[0]
    ens = mem_n * members
    me, tile = lax.axis_index("mem"), lax.axis_index("tile")
    ext = rows + 2 * HALO

    def mem_peer(k):
        return lax.rem(me + k, mem_n)

    def tile_peer(k):
        return lax.rem(tile + k, tile_n)

    barrier = pltpu.get_barrier_semaphore()
    for k in range(1, mem_n):
        pl.semaphore_signal(barrier, inc=1, device_id={"mem": mem_peer(k)}, device_id_type=pl.DeviceIdType.MESH)
    for k in range(1, tile_n):
        pl.semaphore_signal(barrier, inc=1, device_id={"tile": tile_peer(k)}, device_id_type=pl.DeviceIdType.MESH)
    def remote(src, dst, send, recv, axis, index):
        return pltpu.make_async_remote_copy(
            src_ref=src, dst_ref=dst, send_sem=send, recv_sem=recv,
            device_id={axis: index}, device_id_type=pl.DeviceIdType.MESH,
        )

    to_next = remote(
        lat, halo.at[0], halo_send.at[0], halo_recv.at[0], "tile", jnp.minimum(tile + 1, tile_n - 1)
    )
    to_prev = remote(
        lat, halo.at[1], halo_send.at[1], halo_recv.at[1], "tile", jnp.maximum(tile - 1, 0)
    )
    has_next, has_prev = tile < tile_n - 1, tile > 0

    def build_in(layer):
        zero = jnp.zeros((half, hidden), BF16)
        for di in range(3):
            tap = lambda dj: w_in[layer, pl.ds((di * 3 + dj) * half, half), :]
            blocks = ((tap(1), tap(0)), (tap(2), tap(1)), (zero, tap(2)), (tap(0), zero))
            for b, (even, odd) in enumerate(blocks):
                at = pl.ds((di * 4 + b) * half, half)
                big_in[layer, at, pl.ds(0, hidden)] = even
                big_in[layer, at, pl.ds(hidden, hidden)] = odd

    def build_out(layer):
        zero = jnp.zeros((half, hidden), BF16)
        for di in range(3):
            tap = lambda dj: w_out[layer, :, pl.ds((di * 3 + dj) * hidden, hidden)]
            blocks = ((tap(1), tap(2)), (tap(0), tap(1)), (zero, tap(0)), (tap(2), zero))
            for b, (even, odd) in enumerate(blocks):
                at = pl.ds(b * half, half)
                big_out[layer, at, pl.ds(di * 2 * hidden, hidden)] = even
                big_out[layer, at, pl.ds((di * 2 + 1) * hidden, hidden)] = odd

    def build_obs():
        weight = w_obs[...]
        zero = jnp.zeros((obs_ch, half), BF16)
        blocks = []
        for parity in range(2):
            for di in range(3):
                tap = lambda dj: weight[:, (di * 3 + dj) * half : (di * 3 + dj + 1) * half]
                blocks += [[tap(1), tap(2), zero, tap(0)], [tap(0), tap(1), tap(2), zero]][parity]
        spread_ch = iota((obs_lanes, obs_ch), 0) % obs_ch == iota((obs_lanes, obs_ch), 1)
        big_obs[...] = jnp.dot(
            spread_ch.astype(BF16), jnp.concatenate(blocks, axis=1), preferred_element_type=F32
        ).astype(BF16)

    def unfold(slot, source, m):
        for p in range(pairs):
            tile_p = source[m, :, pl.ds(p * lanes, lanes)] if slot is None else source[slot, m, :, pl.ds(p * lanes, lanes)]
            stage[pl.ds(p * rows, rows), :] = tile_p.astype(F32)

    def unfolded(first, count):
        return jnp.concatenate(
            [stage[pl.ds(first + r, pairs, stride=rows), :] for r in range(count)], axis=0
        )

    def take(slot, source, m, first, start, count):
        unfold(slot, source, m)
        wide = unfolded(first, count)
        put(raw, m, start, count, wide.astype(BF16))
        put(frame, m, start, count, norm_frame(wide))

    ones = (iota((2 * lanes, lanes), 0) // half % 2 == iota((2 * lanes, lanes), 1) // half).astype(BF16)

    def norm_frame(x):
        wide = x.astype(F32)
        square = wide * wide
        high = square.astype(BF16)
        low = (square - high.astype(F32)).astype(BF16)
        total = jnp.dot(jnp.concatenate([high, low], axis=1), ones, preferred_element_type=F32)
        normed = wide * lax.rsqrt(total * (1.0 / half) + EPS)
        return with_sides(normed)

    def with_sides(v):
        return jnp.concatenate([v, neighbours(v, pairs, half, False)], axis=1).astype(BF16)

    def flat(ref, m, start, count):
        return ref[m, pl.ds(start, count)].reshape(count * pairs, ref.shape[-1])

    def put(ref, m, start, count, value):
        ref[m, pl.ds(start, count)] = value.reshape(count, pairs, ref.shape[-1])

    def taps(ref, m, start, count):
        return jnp.concatenate([flat(ref, m, start + d - 1, count) for d in range(3)], axis=1)

    def conv_in(layer, m, start, count):
        summed = jnp.dot(taps(frame, m, start, count), big_in[layer], preferred_element_type=F32)
        act = 0.5 * summed * (1.0 + jnp.tanh(0.5 * summed))
        put(hid, m, start, count, act.astype(BF16))

    def conv_out(layer, m, start, count, before):
        summed = lax.dot_general(
            taps(hid, m, start, count), big_out[layer], (((1,), (1,)), ((), ())), preferred_element_type=F32
        )
        summed = summed[:, :lanes] + neighbours(summed[:, lanes:], pairs, half, True)
        return (before.astype(F32) + summed).astype(BF16)

    def blank(ref, low, high):
        def clear(start, count):
            ref[:, pl.ds(start, count)] = jnp.zeros((members, count) + ref.shape[2:], BF16)
        pl.when(tile == 0)(lambda: clear(low, HALO - low))
        pl.when(tile == tile_n - 1)(lambda: clear(HALO + rows, high - HALO - rows))

    build_in(0)
    pl.semaphore_wait(barrier, mem_n - 1 + tile_n - 1)
    pl.when(has_next)(lambda: to_next.start())
    pl.when(has_prev)(lambda: to_prev.start())
    for m in range(members):
        take(None, lat, m, 0, HALO, rows)
    for m in range(members):
        conv_in(0, m, HALO + 1, rows - 2)
    build_out(0)
    build_in(1)
    build_out(1)
    build_obs()
    eye = (iota((obs_cols, obs_cols), 0) == iota((obs_cols, obs_cols), 1)).astype(BF16)
    cells_t = lax.dot_general(
        eye, cells[...].astype(F32).astype(BF16), (((1,), (1,)), ((), ())), preferred_element_type=F32
    ).astype(jnp.int32)

    pl.when(has_prev)(lambda: to_next.wait_recv())
    pl.when(has_next)(lambda: to_prev.wait_recv())

    @pl.when(tile == 0)
    def _():
        halo[0] = jnp.zeros(halo.shape[1:], BF16)

    @pl.when(tile == tile_n - 1)
    def _():
        halo[1] = jnp.zeros(halo.shape[1:], BF16)

    for m in range(members):
        take(0, halo, m, rows - HALO, 0, HALO)
        take(1, halo, m, 0, HALO + rows, HALO)
        conv_in(0, m, 1, HALO)
        conv_in(0, m, HALO + rows - 1, HALO)
    blank(hid, 1, ext - 1)
    for m in range(members):
        put(cur, m, 2, ext - 4, conv_out(0, m, 2, ext - 4, flat(raw, m, 2, ext - 4)))
    blank(cur, 2, ext - 2)
    for m in range(members):
        put(frame, m, 2, ext - 4, norm_frame(flat(cur, m, 2, ext - 4)))
        conv_in(1, m, 3, ext - 6)
    blank(hid, 3, ext - 3)

    step = 2 if mem_n % 2 == 0 else 1
    sibling = me + 1 - 2 * lax.rem(me, 2)
    edge_next, edge_prev, bulk, forwards = [], [], [], []

    def share(m):
        block = gathered.at[me, m]
        for k in range(step, mem_n, step):
            bulk.append(remote(block, block, bulk_send.at[k, m], bulk_recv.at[me, m], "mem", mem_peer(k)))
        if step == 2:
            bulk.append(remote(block, block, bulk_send.at[0, m], bulk_recv.at[me, m], "mem", sibling))
        for copy in bulk[-(mem_n // step if step == 2 else mem_n - 1):]:
            copy.start()

    def arrived(k, m):
        j = mem_peer(k)
        block = gathered.at[j, m]
        remote(block, block, bulk_send.at[0, m], bulk_recv.at[j, m], "mem", j).wait_recv()

    def pass_on(m):
        if step == 2:
            for k in range(2, mem_n, 2):
                arrived(k, m)
                j = mem_peer(k)
                block = gathered.at[j, m]
                copy = remote(block, block, fwd_send.at[k, m], bulk_recv.at[j, m], "mem", sibling)
                copy.start()
                forwards.append(copy)

    early = (members + 1) // 2
    for m in range(members):
        done = conv_out(1, m, HALO, rows, flat(cur, m, HALO, rows))
        gathered[me, m] = done.reshape(rows, pairs, lanes)
        edge_next.append(remote(
            gathered.at[me, m, rows - 1], edge.at[0, m], edge_send.at[0, m], edge_recv.at[0, m],
            "tile", jnp.minimum(tile + 1, tile_n - 1),
        ))
        edge_prev.append(remote(
            gathered.at[me, m, 0], edge.at[1, m], edge_send.at[1, m], edge_recv.at[1, m],
            "tile", jnp.maximum(tile - 1, 0),
        ))
        pl.when(has_next)(lambda: edge_next[m].start())
        pl.when(has_prev)(lambda: edge_prev[m].start())
        if m < early:
            share(m)

    for m in range(members):
        put(frame, m, HALO, rows, with_sides(gathered[me, m].astype(F32).reshape(rows * pairs, lanes)))
    column = 2 * iota((obs_cols, pairs), 1)
    wide = 12 * half

    def observe(r):
        here = cells_t[:, r : r + 1]
        pick = jnp.concatenate([(here == column), (here == column + 1)], axis=0).astype(BF16)
        around = jnp.concatenate([taps(frame, m, HALO + r, 1) for m in range(members)], axis=1)
        got = jnp.dot(pick, around, preferred_element_type=F32).astype(BF16)
        for m in range(members):
            part = got[:, m * wide : (m + 1) * wide]
            at = pl.ds((m * rows + r) * obs_cols, obs_cols)
            patch[at, pl.ds(0, wide)] = part[:obs_cols]
            patch[at, pl.ds(wide, wide)] = part[obs_cols:]

    for r in range(1, rows - 1):
        observe(r)
    for m in range(members):
        pl.when(has_prev)(lambda: edge_next[m].wait_recv())
        pl.when(has_next)(lambda: edge_prev[m].wait_recv())

    @pl.when(tile == 0)
    def _():
        edge[0] = jnp.zeros(edge.shape[1:], BF16)

    @pl.when(tile == tile_n - 1)
    def _():
        edge[1] = jnp.zeros(edge.shape[1:], BF16)

    for m in range(members):
        frame[m, HALO - 1] = with_sides(edge[0, m].astype(F32))
        frame[m, HALO + rows] = with_sides(edge[1, m].astype(F32))
    for r in sorted({0, rows - 1}):
        observe(r)
    spread_pred = lax.dot_general(
        patch[...], big_obs[...], (((1,), (1,)), ((), ())), preferred_element_type=F32
    )
    spread_pred = spread_pred.reshape(members * rows, obs_cols, obs_lanes)
    own = iota(spread_pred.shape, 1) == iota(spread_pred.shape, 2) // obs_ch
    per = members * rows
    mine_at = pl.ds(pl.multiple_of(me * per, per), per)
    preds[mine_at, :] = jnp.sum(jnp.where(own, spread_pred, 0.0), axis=1)

    pred_copies = [
        remote(preds.at[mine_at], preds.at[mine_at], pred_send.at[k], pred_recv.at[me], "mem", mem_peer(k))
        for k in range(1, mem_n)
    ]
    for copy in pred_copies:
        copy.start()
    for m in range(early, members):
        share(m)
    for m in range(early):
        pass_on(m)
    for k in range(1, mem_n):
        j = mem_peer(k)
        block = preds.at[pl.ds(pl.multiple_of(j * per, per), per)]
        remote(block, block, pred_send.at[k], pred_recv.at[j], "mem", j).wait_recv()

    left, right = [], []
    for c in range(0, obs_lanes, 128):
        chunks[c // 128] = preds[:, pl.ds(c, 128)]
    for r in range(rows):
        for c in range(0, obs_lanes, 128):
            at = pl.ds(c, 128)
            here = chunks[c // 128, pl.ds(r, ens, stride=rows), :]
            mean = jnp.sum(here, axis=0, keepdims=True) * (1.0 / ens)
            left.append((here - mean) * precision[pl.ds(r, 1), at])
            right.append(values[pl.ds(r, 1), at] - here)
    part = lax.dot_general(
        jnp.concatenate(left, axis=1), jnp.concatenate(right, axis=1), (((1,), (1,)), ((), ())),
        precision=HIGHEST, preferred_element_type=F32,
    )
    covs[tile] = jnp.concatenate([part, jnp.zeros((ens, covs.shape[2] - ens), F32)], axis=1)
    cov_copies = [
        remote(covs.at[tile], covs.at[tile], cov_send.at[k], cov_recv.at[tile], "tile", tile_peer(k))
        for k in range(1, tile_n)
    ]
    for copy in cov_copies:
        copy.start()

    for m in range(early, members):
        pass_on(m)
    for k in range(1, tile_n):
        j = tile_peer(k)
        remote(covs.at[j], covs.at[j], cov_send.at[k], cov_recv.at[j], "tile", j).wait_recv()
    cov = covs[0]
    for j in range(1, tile_n):
        cov = cov + covs[j]
    cov = cov[:, :ens] * (1.0 / (rows * tile_n * obs_lanes))
    cov_out[...] = cov
    centred = GUIDE_STEP * (cov - jnp.mean(cov, axis=0, keepdims=True))
    factors = []
    for q in range(members):
        mine = iota((ens, ens), 1) == me * members + q
        column_q = jnp.sum(jnp.where(mine, centred, 0.0), axis=1, keepdims=True)
        factors.append(jnp.broadcast_to(column_q, (ens, lanes)))

    for k in range(1, mem_n, step):
        for m in range(members):
            arrived(k, m)
    for r in range(rows):
        acc = [gathered[me, q, r].astype(F32) for q in range(members)]
        for j in range(ens):
            value = gathered[j // members, j % members, r].astype(F32)
            for q in range(members):
                acc[q] = acc[q] + factors[q][j : j + 1] * value
        for q in range(members):
            out[q, r] = acc[q]

    pl.when(has_next)(lambda: to_next.wait_send())
    pl.when(has_prev)(lambda: to_prev.wait_send())
    for m in range(members):
        pl.when(has_next)(lambda: edge_next[m].wait_send())
        pl.when(has_prev)(lambda: edge_prev[m].wait_send())
    for copy in bulk + pred_copies + cov_copies + forwards:
        copy.wait_send()


def per_device(sizes, latents, in_weight, out_weight, observe_weight, obs_cells, obs_values, obs_precision):
    mem_n, tile_n = sizes
    members, rows, flat_count = latents.shape
    half = observe_weight.shape[0] // 9
    lanes = 2 * half
    pairs = flat_count // lanes
    hidden = in_weight.shape[2]
    obs_cols, obs_lanes = obs_cells.shape[1], obs_values.shape[1]
    ens = mem_n * members
    ext = rows + 2 * HALO
    vmem = pl.BlockSpec(memory_space=pltpu.VMEM)
    dma = pltpu.SemaphoreType.DMA
    analysis, covariance = pl.pallas_call(
        functools.partial(kernel, sizes),
        out_shape=(
            jax.ShapeDtypeStruct((members, rows, pairs, lanes), F32),
            jax.ShapeDtypeStruct((ens, ens), F32),
        ),
        in_specs=[vmem] * 7,
        out_specs=(vmem, vmem),
        scratch_shapes=[
            pltpu.VMEM((2, members, rows, flat_count), BF16),
            pltpu.VMEM((pairs * rows, lanes), F32),
            pltpu.VMEM((members, ext, pairs, lanes), BF16),
            pltpu.VMEM((members, ext, pairs, 2 * lanes), BF16),
            pltpu.VMEM((members, ext, pairs, 2 * hidden), BF16),
            pltpu.VMEM((members, ext, pairs, lanes), BF16),
            pltpu.VMEM((2, 12 * half, 2 * hidden), BF16),
            pltpu.VMEM((2, 2 * lanes, 6 * hidden), BF16),
            pltpu.VMEM((obs_lanes, 24 * half), BF16),
            pltpu.VMEM((members * rows * obs_cols, 24 * half), BF16),
            pltpu.VMEM((mem_n, members, rows, pairs, lanes), BF16),
            pltpu.VMEM((2, members, pairs, lanes), BF16),
            pltpu.VMEM((mem_n * members * rows, obs_lanes), F32),
            pltpu.VMEM((obs_lanes // 128, ens * rows, 128), F32),
            pltpu.VMEM((tile_n, ens, 128), F32),
            dma((2,)), dma((2,)), dma((2, members)), dma((2, members)),
            dma((mem_n,)), dma((mem_n,)),
            dma((mem_n, members)), dma((mem_n, members)), dma((mem_n, members)),
            dma((tile_n,)), dma((tile_n,)),
        ],
        compiler_params=pltpu.CompilerParams(
            collective_id=0, has_side_effects=True, vmem_limit_bytes=48 * 1024 * 1024
        ),
    )(
        latents, in_weight, out_weight.transpose(0, 2, 1), observe_weight.T,
        obs_cells, obs_values, obs_precision,
    )
    return analysis.reshape(members, rows, flat_count), covariance


def solution(mesh):
    in_specs = (
        P("mem", "tile", None), P(), P(), P(), P("tile", None), P("tile", None), P("tile", None),
    )
    out_specs = (P("mem", "tile", None), P())
    sizes = (mesh.shape["mem"], mesh.shape["tile"])
    return jax.shard_map(
        functools.partial(per_device, sizes), mesh=mesh, in_specs=in_specs, out_specs=out_specs, check_vma=False
    )
```

```python
import functools

import jax
import jax.numpy as jnp
from jax import lax
from jax.experimental import pallas as pl
from jax.experimental.pallas import tpu as pltpu
from jax.sharding import PartitionSpec as P

EPS = 1e-06
GUIDE_STEP = 0.5
HALO = 4
BF16 = jnp.bfloat16
F32 = jnp.float32
HIGHEST = lax.Precision.HIGHEST


def iota(shape, axis):
    return lax.broadcasted_iota(jnp.int32, shape, axis)


def neighbours(values, pairs, half, swap):
    count, lanes = values.shape
    pair = iota((1, pairs, lanes), 1)
    low = iota((1, pairs, lanes), 2) < half
    following = pltpu.roll(values, count - 1, 0).reshape(count // pairs, pairs, lanes)
    previous = pltpu.roll(values, 1, 0).reshape(count // pairs, pairs, lanes)
    if swap:
        outside = (low & (pair == 0)) | (~low & (pair == pairs - 1))
        picked = jnp.where(low, previous, following)
    else:
        outside = (low & (pair == pairs - 1)) | (~low & (pair == 0))
        picked = jnp.where(low, following, previous)
    return jnp.where(outside, 0.0, picked).reshape(count, lanes)


def kernel(
    sizes, *refs
):
    mem_n, tile_n = sizes
    operands, (out, cov_out), local, load_sem, rest = refs[:7], refs[7:9], refs[9:16], refs[16], refs[17:]
    lat, w_in, w_out, w_obs, cells, values, precision = local
    (
    halo, stage, raw, frame, hid, cur, big_in, big_out, big_obs, patch, gathered, edge, preds, chunks, covs,
    halo_send, halo_recv, edge_send, edge_recv, pred_send, pred_recv,
    bulk_send, fwd_send, bulk_recv, cov_send, cov_recv,
    ) = rest
    members, rows, flat_count = lat.shape
    half = w_obs.shape[1] // 9
    lanes = 2 * half
    pairs = flat_count // lanes
    hidden = w_in.shape[2]
    obs_cols = cells.shape[1]
    obs_lanes = values.shape[1]
    obs_ch = w_obs.shape[0]
    ens = mem_n * members
    me, tile = lax.axis_index("mem"), lax.axis_index("tile")
    ext = rows + 2 * HALO

    def mem_peer(k):
        return lax.rem(me + k, mem_n)

    def tile_peer(k):
        return lax.rem(tile + k, tile_n)

    loads = [
        pltpu.make_async_copy(source, dest, load_sem.at[i])
        for i, (source, dest) in enumerate(zip(operands, local))
    ]
    for load in loads:
        load.start()
    barrier = pltpu.get_barrier_semaphore()
    for k in range(1, mem_n):
        pl.semaphore_signal(barrier, inc=1, device_id={"mem": mem_peer(k)}, device_id_type=pl.DeviceIdType.MESH)
    for k in range(1, tile_n):
        pl.semaphore_signal(barrier, inc=1, device_id={"tile": tile_peer(k)}, device_id_type=pl.DeviceIdType.MESH)
    def remote(src, dst, send, recv, axis, index):
        return pltpu.make_async_remote_copy(
            src_ref=src, dst_ref=dst, send_sem=send, recv_sem=recv,
            device_id={axis: index}, device_id_type=pl.DeviceIdType.MESH,
        )

    to_next = remote(
        operands[0], halo.at[0], halo_send.at[0], halo_recv.at[0], "tile", jnp.minimum(tile + 1, tile_n - 1)
    )
    to_prev = remote(
        operands[0], halo.at[1], halo_send.at[1], halo_recv.at[1], "tile", jnp.maximum(tile - 1, 0)
    )
    has_next, has_prev = tile < tile_n - 1, tile > 0

    def build_in(layer):
        zero = jnp.zeros((half, hidden), BF16)
        for di in range(3):
            tap = lambda dj: w_in[layer, pl.ds((di * 3 + dj) * half, half), :] * BF16(0.5)
            blocks = ((tap(1), tap(0)), (tap(2), tap(1)), (zero, tap(2)), (tap(0), zero))
            for b, (even, odd) in enumerate(blocks):
                at = pl.ds((di * 4 + b) * half, half)
                big_in[layer, at, pl.ds(0, hidden)] = even
                big_in[layer, at, pl.ds(hidden, hidden)] = odd

    def build_out(layer):
        zero = jnp.zeros((half, hidden), BF16)
        for di in range(3):
            tap = lambda dj: w_out[layer, :, pl.ds((di * 3 + dj) * hidden, hidden)]
            blocks = ((tap(1), tap(2)), (tap(0), tap(1)), (zero, tap(0)), (tap(2), zero))
            for b, (even, odd) in enumerate(blocks):
                at = pl.ds(b * half, half)
                big_out[layer, at, pl.ds(di * 2 * hidden, hidden)] = even
                big_out[layer, at, pl.ds((di * 2 + 1) * hidden, hidden)] = odd

    def build_obs():
        weight = w_obs[...]
        zero = jnp.zeros((obs_ch, half), BF16)
        blocks = []
        for parity in range(2):
            for di in range(3):
                tap = lambda dj: weight[:, (di * 3 + dj) * half : (di * 3 + dj + 1) * half]
                blocks += [[tap(1), tap(2), zero, tap(0)], [tap(0), tap(1), tap(2), zero]][parity]
        same_ch = (iota((obs_ch, obs_ch), 0) == iota((obs_ch, obs_ch), 1)).astype(F32)
        spread_ch = jnp.concatenate([same_ch] * obs_cols, axis=0)
        big_obs[...] = jnp.dot(
            spread_ch.astype(BF16), jnp.concatenate(blocks, axis=1), preferred_element_type=F32
        ).astype(BF16)

    def unfold(slot, source, m):
        for p in range(pairs):
            tile_p = source[m, :, pl.ds(p * lanes, lanes)] if slot is None else source[slot, m, :, pl.ds(p * lanes, lanes)]
            stage[pl.ds(p * rows, rows), :] = tile_p.astype(F32)

    def unfolded(first, count):
        return jnp.concatenate(
            [stage[pl.ds(first + r, pairs, stride=rows), :] for r in range(count)], axis=0
        )

    def take(slot, source, m, first, start, count):
        unfold(slot, source, m)
        wide = unfolded(first, count)
        put(raw, m, start, count, wide.astype(BF16))
        put(frame, m, start, count, norm_frame(wide))

    block = ((iota((lanes, lanes), 0) < half) == (iota((lanes, lanes), 1) < half)).astype(BF16)
    ones = jnp.concatenate([block, block], axis=0)

    def norm_frame(x):
        wide = x.astype(F32)
        square = wide * wide
        high = square.astype(BF16)
        low = (square - high.astype(F32)).astype(BF16)
        total = jnp.dot(jnp.concatenate([high, low], axis=1), ones, preferred_element_type=F32)
        normed = wide * lax.rsqrt(total * (1.0 / half) + EPS)
        return with_sides(normed)

    def with_sides(v):
        return jnp.concatenate([v, neighbours(v, pairs, half, False)], axis=1).astype(BF16)

    def flat(ref, m, start, count):
        return ref[m, pl.ds(start, count)].reshape(count * pairs, ref.shape[-1])

    def put(ref, m, start, count, value):
        ref[m, pl.ds(start, count)] = value.reshape(count, pairs, ref.shape[-1])

    def taps(ref, m, start, count):
        return jnp.concatenate([flat(ref, m, start + d - 1, count) for d in range(3)], axis=1)

    def conv_in(layer, m, start, count):
        summed = jnp.dot(taps(frame, m, start, count), big_in[layer], preferred_element_type=F32)
        act = summed + summed * jnp.tanh(summed)
        put(hid, m, start, count, act.astype(BF16))

    def conv_out(layer, m, start, count, before):
        summed = lax.dot_general(
            taps(hid, m, start, count), big_out[layer], (((1,), (1,)), ((), ())), preferred_element_type=F32
        )
        summed = summed[:, :lanes] + neighbours(summed[:, lanes:], pairs, half, True)
        return (before.astype(F32) + summed).astype(BF16)

    def blank(ref, low, high):
        def clear(start, count):
            ref[:, pl.ds(start, count)] = jnp.zeros((members, count) + ref.shape[2:], BF16)
        pl.when(tile == 0)(lambda: clear(low, HALO - low))
        pl.when(tile == tile_n - 1)(lambda: clear(HALO + rows, high - HALO - rows))

    def each_member(body):
        def step_m(m, carry):
            body(m)
            return carry
        lax.fori_loop(0, members, step_m, 0)

    pl.semaphore_wait(barrier, mem_n - 1 + tile_n - 1)
    pl.when(has_next)(lambda: to_next.start())
    pl.when(has_prev)(lambda: to_prev.start())
    loads[0].wait()
    each_member(lambda m: take(None, lat, m, 0, HALO, rows))
    loads[1].wait()
    build_in(0)
    each_member(lambda m: conv_in(0, m, HALO + 1, rows - 2))
    for load in loads[2:]:
        load.wait()
    build_out(0)
    build_in(1)
    build_out(1)
    build_obs()
    eye = (iota((obs_cols, obs_cols), 0) == iota((obs_cols, obs_cols), 1)).astype(BF16)
    cells_t = lax.dot_general(
        eye, cells[...].astype(F32).astype(BF16), (((1,), (1,)), ((), ())), preferred_element_type=F32
    ).astype(jnp.int32)

    pl.when(has_prev)(lambda: to_next.wait_recv())
    pl.when(has_next)(lambda: to_prev.wait_recv())

    @pl.when(tile == 0)
    def _():
        halo[0] = jnp.zeros(halo.shape[1:], BF16)

    @pl.when(tile == tile_n - 1)
    def _():
        halo[1] = jnp.zeros(halo.shape[1:], BF16)

    def outer_rows(m):
        take(0, halo, m, rows - HALO, 0, HALO)
        take(1, halo, m, 0, HALO + rows, HALO)
        conv_in(0, m, 1, HALO)
        conv_in(0, m, HALO + rows - 1, HALO)

    def first_out(m):
        put(cur, m, 2, ext - 4, conv_out(0, m, 2, ext - 4, flat(raw, m, 2, ext - 4)))

    def second_in(m):
        put(frame, m, 2, ext - 4, norm_frame(flat(cur, m, 2, ext - 4)))
        conv_in(1, m, 3, ext - 6)

    each_member(outer_rows)
    blank(hid, 1, ext - 1)
    each_member(first_out)
    blank(cur, 2, ext - 2)
    each_member(second_in)
    blank(hid, 3, ext - 3)

    step = 2 if mem_n % 2 == 0 else 1
    sibling = me + 1 - 2 * lax.rem(me, 2)
    edge_next, edge_prev, bulk, forwards = [], [], [], []

    def share(m):
        block = gathered.at[me, m]
        for k in range(step, mem_n, step):
            bulk.append(remote(block, block, bulk_send.at[k, m], bulk_recv.at[me, m], "mem", mem_peer(k)))
        if step == 2:
            bulk.append(remote(block, block, bulk_send.at[0, m], bulk_recv.at[me, m], "mem", sibling))
        for copy in bulk[-(mem_n // step if step == 2 else mem_n - 1):]:
            copy.start()

    def arrived(k, m):
        j = mem_peer(k)
        block = gathered.at[j, m]
        remote(block, block, bulk_send.at[0, m], bulk_recv.at[j, m], "mem", j).wait_recv()

    def pass_on(m):
        if step == 2:
            for k in range(2, mem_n, 2):
                arrived(k, m)
                j = mem_peer(k)
                block = gathered.at[j, m]
                copy = remote(block, block, fwd_send.at[k, m], bulk_recv.at[j, m], "mem", sibling)
                copy.start()
                forwards.append(copy)

    early = (members + 1) // 2
    for m in range(members):
        done = conv_out(1, m, HALO, rows, flat(cur, m, HALO, rows))
        gathered[me, m] = done.reshape(rows, pairs, lanes)
        edge_next.append(remote(
            gathered.at[me, m, rows - 1], edge.at[0, m], edge_send.at[0, m], edge_recv.at[0, m],
            "tile", jnp.minimum(tile + 1, tile_n - 1),
        ))
        edge_prev.append(remote(
            gathered.at[me, m, 0], edge.at[1, m], edge_send.at[1, m], edge_recv.at[1, m],
            "tile", jnp.maximum(tile - 1, 0),
        ))
        pl.when(has_next)(lambda: edge_next[m].start())
        pl.when(has_prev)(lambda: edge_prev[m].start())
        if m < early:
            share(m)

    for m in range(members):
        put(frame, m, HALO, rows, with_sides(gathered[me, m].astype(F32).reshape(rows * pairs, lanes)))
    column = 2 * iota((obs_cols, pairs), 1)
    wide = 12 * half

    def observe(r):
        here = cells_t[:, r : r + 1]
        pick = jnp.concatenate([(here == column), (here == column + 1)], axis=0).astype(BF16)
        around = jnp.concatenate([taps(frame, m, HALO + r, 1) for m in range(members)], axis=1)
        got = jnp.dot(pick, around, preferred_element_type=F32).astype(BF16)
        for m in range(members):
            part = got[:, m * wide : (m + 1) * wide]
            at = pl.ds((m * rows + r) * obs_cols, obs_cols)
            patch[at, pl.ds(0, wide)] = part[:obs_cols]
            patch[at, pl.ds(wide, wide)] = part[obs_cols:]

    for r in range(1, rows - 1):
        observe(r)
    for m in range(members):
        pl.when(has_prev)(lambda: edge_next[m].wait_recv())
        pl.when(has_next)(lambda: edge_prev[m].wait_recv())

    @pl.when(tile == 0)
    def _():
        edge[0] = jnp.zeros(edge.shape[1:], BF16)

    @pl.when(tile == tile_n - 1)
    def _():
        edge[1] = jnp.zeros(edge.shape[1:], BF16)

    for m in range(members):
        frame[m, HALO - 1] = with_sides(edge[0, m].astype(F32))
        frame[m, HALO + rows] = with_sides(edge[1, m].astype(F32))
    for r in sorted({0, rows - 1}):
        observe(r)
    spread_pred = lax.dot_general(
        patch[...], big_obs[...], (((1,), (1,)), ((), ())), preferred_element_type=F32
    )
    spread_pred = spread_pred.reshape(members * rows, obs_cols, obs_lanes)
    first_lane = iota((1, obs_cols, obs_lanes), 1) * obs_ch
    lane = iota((1, obs_cols, obs_lanes), 2)
    own = (lane >= first_lane) & (lane < first_lane + obs_ch)
    per = members * rows
    mine_at = pl.ds(pl.multiple_of(me * per, per), per)
    preds[mine_at, :] = jnp.sum(jnp.where(own, spread_pred, 0.0), axis=1)

    pred_copies = [
        remote(preds.at[mine_at], preds.at[mine_at], pred_send.at[k], pred_recv.at[me], "mem", mem_peer(k))
        for k in range(1, mem_n)
    ]
    for copy in pred_copies:
        copy.start()
    for m in range(early, members):
        share(m)
    for m in range(early):
        pass_on(m)
    for k in range(1, mem_n):
        j = mem_peer(k)
        block = preds.at[pl.ds(pl.multiple_of(j * per, per), per)]
        remote(block, block, pred_send.at[k], pred_recv.at[j], "mem", j).wait_recv()

    left, right = [], []
    for c in range(0, obs_lanes, 128):
        chunks[c // 128] = preds[:, pl.ds(c, 128)]
    for r in range(rows):
        for c in range(0, obs_lanes, 128):
            at = pl.ds(c, 128)
            here = chunks[c // 128, pl.ds(r, ens, stride=rows), :]
            mean = jnp.sum(here, axis=0, keepdims=True) * (1.0 / ens)
            left.append((here - mean) * precision[pl.ds(r, 1), at])
            right.append(values[pl.ds(r, 1), at] - here)
    part = lax.dot_general(
        jnp.concatenate(left, axis=1), jnp.concatenate(right, axis=1), (((1,), (1,)), ((), ())),
        precision=HIGHEST, preferred_element_type=F32,
    )
    covs[tile] = jnp.concatenate([part, jnp.zeros((ens, covs.shape[2] - ens), F32)], axis=1)
    cov_copies = [
        remote(covs.at[tile], covs.at[tile], cov_send.at[k], cov_recv.at[tile], "tile", tile_peer(k))
        for k in range(1, tile_n)
    ]
    for copy in cov_copies:
        copy.start()

    for m in range(early, members):
        pass_on(m)
    for k in range(1, tile_n):
        j = tile_peer(k)
        remote(covs.at[j], covs.at[j], cov_send.at[k], cov_recv.at[j], "tile", j).wait_recv()
    cov = covs[0]
    for j in range(1, tile_n):
        cov = cov + covs[j]
    cov = cov[:, :ens] * (1.0 / (rows * tile_n * obs_lanes))
    cov_out[...] = cov
    centred = GUIDE_STEP * (cov - jnp.mean(cov, axis=0, keepdims=True))
    factors = []
    for q in range(members):
        mine = iota((ens, ens), 1) == me * members + q
        column_q = jnp.sum(jnp.where(mine, centred, 0.0), axis=1, keepdims=True)
        factors.append(jnp.broadcast_to(column_q, (ens, lanes)))

    for k in range(1, mem_n, step):
        for m in range(members):
            arrived(k, m)
    def update_row(r, carry):
        acc = [gathered[me, q, r].astype(F32) for q in range(members)]
        for j in range(ens):
            value = gathered[j // members, j % members, r].astype(F32)
            for q in range(members):
                acc[q] = acc[q] + factors[q][j : j + 1] * value
        for q in range(members):
            out[q, r] = acc[q]
        return carry

    lax.fori_loop(0, rows, update_row, 0)

    pl.when(has_next)(lambda: to_next.wait_send())
    pl.when(has_prev)(lambda: to_prev.wait_send())
    for m in range(members):
        pl.when(has_next)(lambda: edge_next[m].wait_send())
        pl.when(has_prev)(lambda: edge_prev[m].wait_send())
    for copy in bulk + pred_copies + cov_copies + forwards:
        copy.wait_send()


def per_device(sizes, latents, in_weight, out_weight, observe_weight, obs_cells, obs_values, obs_precision):
    mem_n, tile_n = sizes
    members, rows, flat_count = latents.shape
    half = observe_weight.shape[0] // 9
    lanes = 2 * half
    pairs = flat_count // lanes
    hidden = in_weight.shape[2]
    obs_cols, obs_lanes = obs_cells.shape[1], obs_values.shape[1]
    ens = mem_n * members
    ext = rows + 2 * HALO
    operands = (
        latents, in_weight, out_weight.transpose(0, 2, 1), observe_weight.T, obs_cells, obs_values, obs_precision
    )
    vmem = pl.BlockSpec(memory_space=pltpu.VMEM)
    dma = pltpu.SemaphoreType.DMA
    analysis, covariance = pl.pallas_call(
        functools.partial(kernel, sizes),
        out_shape=(
            jax.ShapeDtypeStruct((members, rows, pairs, lanes), F32),
            jax.ShapeDtypeStruct((ens, ens), F32),
        ),
        in_specs=[pl.BlockSpec(memory_space=pltpu.HBM)] * 7,
        out_specs=(vmem, vmem),
        scratch_shapes=[pltpu.VMEM(x.shape, x.dtype) for x in operands] + [
            dma((7,)),
            pltpu.VMEM((2, members, rows, flat_count), BF16),
            pltpu.VMEM((pairs * rows, lanes), F32),
            pltpu.VMEM((members, ext, pairs, lanes), BF16),
            pltpu.VMEM((members, ext, pairs, 2 * lanes), BF16),
            pltpu.VMEM((members, ext, pairs, 2 * hidden), BF16),
            pltpu.VMEM((members, ext, pairs, lanes), BF16),
            pltpu.VMEM((2, 12 * half, 2 * hidden), BF16),
            pltpu.VMEM((2, 2 * lanes, 6 * hidden), BF16),
            pltpu.VMEM((obs_lanes, 24 * half), BF16),
            pltpu.VMEM((members * rows * obs_cols, 24 * half), BF16),
            pltpu.VMEM((mem_n, members, rows, pairs, lanes), BF16),
            pltpu.VMEM((2, members, pairs, lanes), BF16),
            pltpu.VMEM((mem_n * members * rows, obs_lanes), F32),
            pltpu.VMEM((obs_lanes // 128, ens * rows, 128), F32),
            pltpu.VMEM((tile_n, ens, 128), F32),
            dma((2,)), dma((2,)), dma((2, members)), dma((2, members)),
            dma((mem_n,)), dma((mem_n,)),
            dma((mem_n, members)), dma((mem_n, members)), dma((mem_n, members)),
            dma((tile_n,)), dma((tile_n,)),
        ],
        compiler_params=pltpu.CompilerParams(
            collective_id=0, has_side_effects=True, vmem_limit_bytes=32 * 1024 * 1024
        ),
    )(*operands)
    return analysis.reshape(members, rows, flat_count), covariance


def solution(mesh):
    in_specs = (
        P("mem", "tile", None), P(), P(), P(), P("tile", None), P("tile", None), P("tile", None),
    )
    out_specs = (P("mem", "tile", None), P())
    sizes = (mesh.shape["mem"], mesh.shape["tile"])
    return jax.shard_map(
        functools.partial(per_device, sizes), mesh=mesh, in_specs=in_specs, out_specs=out_specs, check_vma=False
    )
```

```python
import functools

import jax
import jax.numpy as jnp
from jax import lax
from jax.experimental import pallas as pl
from jax.experimental.pallas import tpu as pltpu
from jax.sharding import PartitionSpec as P

EPS = 1e-06
GUIDE_STEP = 0.5
HALO = 4
BF16 = jnp.bfloat16
F32 = jnp.float32
HIGHEST = lax.Precision.HIGHEST


def iota(shape, axis):
    return lax.broadcasted_iota(jnp.int32, shape, axis)


def neighbours(values, pairs, half, swap):
    count, lanes = values.shape
    pair = iota((1, pairs, lanes), 1)
    low = iota((1, pairs, lanes), 2) < half
    following = pltpu.roll(values, count - 1, 0).reshape(count // pairs, pairs, lanes)
    previous = pltpu.roll(values, 1, 0).reshape(count // pairs, pairs, lanes)
    if swap:
        outside = (low & (pair == 0)) | (~low & (pair == pairs - 1))
        picked = jnp.where(low, previous, following)
    else:
        outside = (low & (pair == pairs - 1)) | (~low & (pair == 0))
        picked = jnp.where(low, following, previous)
    return jnp.where(outside, 0.0, picked).reshape(count, lanes)


def kernel(
    sizes, *refs
):
    mem_n, tile_n = sizes
    operands, (out, cov_out), local, load_sem, rest = refs[:7], refs[7:9], refs[9:16], refs[16], refs[17:]
    lat, w_in, w_out, w_obs, cells, values, precision = local
    (
    halo, stage, raw, frame, hid, cur, big_in, big_out, big_obs, patch, gathered, edge, preds, chunks, covs,
    halo_send, halo_recv, edge_send, edge_recv, pred_send, pred_recv,
    bulk_send, fwd_send, bulk_recv, cov_send, cov_recv,
    ) = rest
    members, rows, flat_count = lat.shape
    half = w_obs.shape[1] // 9
    lanes = 2 * half
    pairs = flat_count // lanes
    hidden = w_in.shape[2]
    obs_cols = cells.shape[1]
    obs_lanes = values.shape[1]
    obs_ch = w_obs.shape[0]
    ens = mem_n * members
    me, tile = lax.axis_index("mem"), lax.axis_index("tile")
    ext = rows + 2 * HALO

    def mem_peer(k):
        return lax.rem(me + k, mem_n)

    def tile_peer(k):
        return lax.rem(tile + k, tile_n)

    loads = [
        pltpu.make_async_copy(source, dest, load_sem.at[i])
        for i, (source, dest) in enumerate(zip(operands, local))
    ]
    for load in loads:
        load.start()
    barrier = pltpu.get_barrier_semaphore()
    for k in range(1, mem_n):
        pl.semaphore_signal(barrier, inc=1, device_id={"mem": mem_peer(k)}, device_id_type=pl.DeviceIdType.MESH)
    for k in range(1, tile_n):
        pl.semaphore_signal(barrier, inc=1, device_id={"tile": tile_peer(k)}, device_id_type=pl.DeviceIdType.MESH)
    def remote(src, dst, send, recv, axis, index):
        return pltpu.make_async_remote_copy(
            src_ref=src, dst_ref=dst, send_sem=send, recv_sem=recv,
            device_id={axis: index}, device_id_type=pl.DeviceIdType.MESH,
        )

    to_next = remote(
        operands[0], halo.at[0], halo_send.at[0], halo_recv.at[0], "tile", jnp.minimum(tile + 1, tile_n - 1)
    )
    to_prev = remote(
        operands[0], halo.at[1], halo_send.at[1], halo_recv.at[1], "tile", jnp.maximum(tile - 1, 0)
    )
    has_next, has_prev = tile < tile_n - 1, tile > 0

    def build_in(layer):
        zero = jnp.zeros((half, hidden), BF16)
        for di in range(3):
            tap = lambda dj: w_in[layer, pl.ds((di * 3 + dj) * half, half), :] * BF16(0.5)
            blocks = ((tap(1), tap(0)), (tap(2), tap(1)), (zero, tap(2)), (tap(0), zero))
            for b, (even, odd) in enumerate(blocks):
                at = pl.ds((di * 4 + b) * half, half)
                big_in[layer, at, pl.ds(0, hidden)] = even
                big_in[layer, at, pl.ds(hidden, hidden)] = odd

    def build_out(layer):
        zero = jnp.zeros((half, hidden), BF16)
        for di in range(3):
            tap = lambda dj: w_out[layer, :, pl.ds((di * 3 + dj) * hidden, hidden)]
            blocks = ((tap(1), tap(2)), (tap(0), tap(1)), (zero, tap(0)), (tap(2), zero))
            for b, (even, odd) in enumerate(blocks):
                at = pl.ds(b * half, half)
                big_out[layer, at, pl.ds(di * 2 * hidden, hidden)] = even
                big_out[layer, at, pl.ds((di * 2 + 1) * hidden, hidden)] = odd

    def build_obs():
        weight = w_obs[...]
        zero = jnp.zeros((obs_ch, half), BF16)
        blocks = []
        for parity in range(2):
            for di in range(3):
                tap = lambda dj: weight[:, (di * 3 + dj) * half : (di * 3 + dj + 1) * half]
                blocks += [[tap(1), tap(2), zero, tap(0)], [tap(0), tap(1), tap(2), zero]][parity]
        same_ch = (iota((obs_ch, obs_ch), 0) == iota((obs_ch, obs_ch), 1)).astype(F32)
        spread_ch = jnp.concatenate([same_ch] * obs_cols, axis=0)
        big_obs[...] = jnp.dot(
            spread_ch.astype(BF16), jnp.concatenate(blocks, axis=1), preferred_element_type=F32
        ).astype(BF16)

    def unfold(slot, source, m):
        for p in range(pairs):
            tile_p = source[m, :, pl.ds(p * lanes, lanes)] if slot is None else source[slot, m, :, pl.ds(p * lanes, lanes)]
            stage[pl.ds(p * rows, rows), :] = tile_p.astype(F32)

    def unfolded(first, count):
        return jnp.concatenate(
            [stage[pl.ds(first + r, pairs, stride=rows), :] for r in range(count)], axis=0
        )

    def take(slot, source, m, first, start, count):
        unfold(slot, source, m)
        wide = unfolded(first, count)
        put(raw, m, start, count, wide.astype(BF16))
        put(frame, m, start, count, norm_frame(wide))

    block = ((iota((lanes, lanes), 0) < half) == (iota((lanes, lanes), 1) < half)).astype(BF16)
    ones = jnp.concatenate([block, block], axis=0)

    def norm_frame(x):
        wide = x.astype(F32)
        square = wide * wide
        high = square.astype(BF16)
        low = (square - high.astype(F32)).astype(BF16)
        total = jnp.dot(jnp.concatenate([high, low], axis=1), ones, preferred_element_type=F32)
        normed = wide * lax.rsqrt(total * (1.0 / half) + EPS)
        return with_sides(normed)

    def with_sides(v):
        return jnp.concatenate([v, neighbours(v, pairs, half, False)], axis=1).astype(BF16)

    def flat(ref, m, start, count):
        return ref[m, pl.ds(start, count)].reshape(count * pairs, ref.shape[-1])

    def put(ref, m, start, count, value):
        ref[m, pl.ds(start, count)] = value.reshape(count, pairs, ref.shape[-1])

    def taps(ref, m, start, count):
        return jnp.concatenate([flat(ref, m, start + d - 1, count) for d in range(3)], axis=1)

    def conv_in(layer, m, start, count):
        summed = jnp.dot(taps(frame, m, start, count), big_in[layer], preferred_element_type=F32)
        act = summed + summed * jnp.tanh(summed)
        put(hid, m, start, count, act.astype(BF16))

    def conv_sum(layer, lhs, before):
        summed = lax.dot_general(
            lhs, big_out[layer], (((1,), (1,)), ((), ())), preferred_element_type=F32
        )
        summed = summed[:, :lanes] + neighbours(summed[:, lanes:], pairs, half, True)
        return (before.astype(F32) + summed).astype(BF16)

    def conv_out(layer, m, start, count, before):
        return conv_sum(layer, taps(hid, m, start, count), before)

    def blank(ref, low, high):
        def clear(start, count):
            ref[:, pl.ds(start, count)] = jnp.zeros((members, count) + ref.shape[2:], BF16)
        pl.when(tile == 0)(lambda: clear(low, HALO - low))
        pl.when(tile == tile_n - 1)(lambda: clear(HALO + rows, high - HALO - rows))

    def each_member(body):
        def step_m(m, carry):
            body(m)
            return carry
        lax.fori_loop(0, members, step_m, 0)

    pl.semaphore_wait(barrier, mem_n - 1 + tile_n - 1)
    pl.when(has_next)(lambda: to_next.start())
    pl.when(has_prev)(lambda: to_prev.start())
    loads[0].wait()
    each_member(lambda m: take(None, lat, m, 0, HALO, rows))
    loads[1].wait()
    build_in(0)
    each_member(lambda m: conv_in(0, m, HALO + 1, rows - 2))
    for load in loads[2:]:
        load.wait()
    build_out(0)
    build_in(1)
    build_out(1)
    build_obs()
    eye = (iota((obs_cols, obs_cols), 0) == iota((obs_cols, obs_cols), 1)).astype(BF16)
    cells_t = lax.dot_general(
        eye, cells[...].astype(F32).astype(BF16), (((1,), (1,)), ((), ())), preferred_element_type=F32
    ).astype(jnp.int32)

    pl.when(has_prev)(lambda: to_next.wait_recv())
    pl.when(has_next)(lambda: to_prev.wait_recv())

    @pl.when(tile == 0)
    def _():
        halo[0] = jnp.zeros(halo.shape[1:], BF16)

    @pl.when(tile == tile_n - 1)
    def _():
        halo[1] = jnp.zeros(halo.shape[1:], BF16)

    def outer_rows(m):
        take(0, halo, m, rows - HALO, 0, HALO)
        take(1, halo, m, 0, HALO + rows, HALO)
        conv_in(0, m, 1, HALO)
        conv_in(0, m, HALO + rows - 1, HALO)

    def first_out(m):
        put(cur, m, 2, ext - 4, conv_out(0, m, 2, ext - 4, flat(raw, m, 2, ext - 4)))

    def second_in(m):
        put(frame, m, 2, ext - 4, norm_frame(flat(cur, m, 2, ext - 4)))
        conv_in(1, m, 3, ext - 6)

    each_member(outer_rows)
    blank(hid, 1, ext - 1)
    each_member(first_out)
    blank(cur, 2, ext - 2)
    each_member(second_in)
    blank(hid, 3, ext - 3)

    step = 2 if mem_n % 2 == 0 else 1
    sibling = me + 1 - 2 * lax.rem(me, 2)
    edge_next, edge_prev, bulk, forwards = [], [], [], []

    def share(m):
        block = gathered.at[me, m]
        for k in range(step, mem_n, step):
            bulk.append(remote(block, block, bulk_send.at[k, m], bulk_recv.at[me, m], "mem", mem_peer(k)))
        if step == 2:
            bulk.append(remote(block, block, bulk_send.at[0, m], bulk_recv.at[me, m], "mem", sibling))
        for copy in bulk[-(mem_n // step if step == 2 else mem_n - 1):]:
            copy.start()

    def arrived(k, m):
        j = mem_peer(k)
        block = gathered.at[j, m]
        remote(block, block, bulk_send.at[0, m], bulk_recv.at[j, m], "mem", j).wait_recv()

    def pass_on(m):
        if step == 2:
            for k in range(2, mem_n, 2):
                arrived(k, m)
                j = mem_peer(k)
                block = gathered.at[j, m]
                copy = remote(block, block, fwd_send.at[k, m], bulk_recv.at[j, m], "mem", sibling)
                copy.start()
                forwards.append(copy)

    early = (members + 1) // 2

    def finish(picked):
        lhs = jnp.concatenate([taps(hid, m, HALO + r, count) for m, r, count in picked], axis=0)
        before = jnp.concatenate([flat(cur, m, HALO + r, count) for m, r, count in picked], axis=0)
        done = conv_sum(1, lhs, before)
        sides = with_sides(done.astype(F32))
        at = 0
        for m, r, count in picked:
            end = at + count * pairs
            gathered[me, m, pl.ds(r, count)] = done[at:end].reshape(count, pairs, lanes)
            put(frame, m, HALO + r, count, sides[at:end])
            at = end

    finish([(m, r, 1) for m in range(members) for r in sorted({0, rows - 1})])
    for m in range(members):
        edge_next.append(remote(
            gathered.at[me, m, rows - 1], edge.at[0, m], edge_send.at[0, m], edge_recv.at[0, m],
            "tile", jnp.minimum(tile + 1, tile_n - 1),
        ))
        edge_prev.append(remote(
            gathered.at[me, m, 0], edge.at[1, m], edge_send.at[1, m], edge_recv.at[1, m],
            "tile", jnp.maximum(tile - 1, 0),
        ))
        pl.when(has_next)(lambda: edge_next[m].start())
        pl.when(has_prev)(lambda: edge_prev[m].start())
    finish([(m, 1, rows - 2) for m in range(members)])
    for m in range(early):
        share(m)

    column = 2 * iota((obs_cols, pairs), 1)
    wide = 12 * half

    def observe(r):
        here = cells_t[:, r : r + 1]
        pick = jnp.concatenate([(here == column), (here == column + 1)], axis=0).astype(BF16)
        around = jnp.concatenate([taps(frame, m, HALO + r, 1) for m in range(members)], axis=1)
        got = jnp.dot(pick, around, preferred_element_type=F32).astype(BF16)
        for m in range(members):
            part = got[:, m * wide : (m + 1) * wide]
            at = pl.ds((m * rows + r) * obs_cols, obs_cols)
            patch[at, pl.ds(0, wide)] = part[:obs_cols]
            patch[at, pl.ds(wide, wide)] = part[obs_cols:]

    for r in range(1, rows - 1):
        observe(r)
    for m in range(members):
        pl.when(has_prev)(lambda: edge_next[m].wait_recv())
        pl.when(has_next)(lambda: edge_prev[m].wait_recv())

    @pl.when(tile == 0)
    def _():
        edge[0] = jnp.zeros(edge.shape[1:], BF16)

    @pl.when(tile == tile_n - 1)
    def _():
        edge[1] = jnp.zeros(edge.shape[1:], BF16)

    for m in range(members):
        frame[m, HALO - 1] = with_sides(edge[0, m].astype(F32))
        frame[m, HALO + rows] = with_sides(edge[1, m].astype(F32))
    for r in sorted({0, rows - 1}):
        observe(r)
    spread_pred = lax.dot_general(
        patch[...], big_obs[...], (((1,), (1,)), ((), ())), preferred_element_type=F32
    )
    spread_pred = spread_pred.reshape(members * rows, obs_cols, obs_lanes)
    first_lane = iota((1, obs_cols, obs_lanes), 1) * obs_ch
    lane = iota((1, obs_cols, obs_lanes), 2)
    own = (lane >= first_lane) & (lane < first_lane + obs_ch)
    per = members * rows
    mine_at = pl.ds(pl.multiple_of(me * per, per), per)
    preds[mine_at, :] = jnp.sum(jnp.where(own, spread_pred, 0.0), axis=1)

    pred_copies = [
        remote(preds.at[mine_at], preds.at[mine_at], pred_send.at[k], pred_recv.at[me], "mem", mem_peer(k))
        for k in range(1, mem_n)
    ]
    for copy in pred_copies:
        copy.start()
    for m in range(early, members):
        share(m)
    for m in range(early):
        pass_on(m)
    for k in range(1, mem_n):
        j = mem_peer(k)
        block = preds.at[pl.ds(pl.multiple_of(j * per, per), per)]
        remote(block, block, pred_send.at[k], pred_recv.at[j], "mem", j).wait_recv()

    left, right = [], []
    for c in range(0, obs_lanes, 128):
        chunks[c // 128] = preds[:, pl.ds(c, 128)]
    for r in range(rows):
        for c in range(0, obs_lanes, 128):
            at = pl.ds(c, 128)
            here = chunks[c // 128, pl.ds(r, ens, stride=rows), :]
            mean = jnp.sum(here, axis=0, keepdims=True) * (1.0 / ens)
            left.append((here - mean) * precision[pl.ds(r, 1), at])
            right.append(values[pl.ds(r, 1), at] - here)
    part = lax.dot_general(
        jnp.concatenate(left, axis=1), jnp.concatenate(right, axis=1), (((1,), (1,)), ((), ())),
        precision=HIGHEST, preferred_element_type=F32,
    )
    covs[tile] = jnp.concatenate([part, jnp.zeros((ens, covs.shape[2] - ens), F32)], axis=1)
    cov_copies = [
        remote(covs.at[tile], covs.at[tile], cov_send.at[k], cov_recv.at[tile], "tile", tile_peer(k))
        for k in range(1, tile_n)
    ]
    for copy in cov_copies:
        copy.start()

    for m in range(early, members):
        pass_on(m)
    for k in range(1, tile_n):
        j = tile_peer(k)
        remote(covs.at[j], covs.at[j], cov_send.at[k], cov_recv.at[j], "tile", j).wait_recv()
    cov = covs[0]
    for j in range(1, tile_n):
        cov = cov + covs[j]
    cov = cov[:, :ens] * (1.0 / (rows * tile_n * obs_lanes))
    cov_out[...] = cov
    centred = GUIDE_STEP * (cov - jnp.mean(cov, axis=0, keepdims=True))
    factors = []
    for q in range(members):
        mine = iota((ens, ens), 1) == me * members + q
        column_q = jnp.sum(jnp.where(mine, centred, 0.0), axis=1, keepdims=True)
        factors.append(jnp.broadcast_to(column_q, (ens, lanes)))

    for k in range(1, mem_n, step):
        for m in range(members):
            arrived(k, m)
    def update_row(r, carry):
        acc = [gathered[me, q, r].astype(F32) for q in range(members)]
        for j in range(ens):
            value = gathered[j // members, j % members, r].astype(F32)
            for q in range(members):
                acc[q] = acc[q] + factors[q][j : j + 1] * value
        for q in range(members):
            out[q, r] = acc[q]
        return carry

    lax.fori_loop(0, rows, update_row, 0)

    pl.when(has_next)(lambda: to_next.wait_send())
    pl.when(has_prev)(lambda: to_prev.wait_send())
    for m in range(members):
        pl.when(has_next)(lambda: edge_next[m].wait_send())
        pl.when(has_prev)(lambda: edge_prev[m].wait_send())
    for copy in bulk + pred_copies + cov_copies + forwards:
        copy.wait_send()


def per_device(sizes, latents, in_weight, out_weight, observe_weight, obs_cells, obs_values, obs_precision):
    mem_n, tile_n = sizes
    members, rows, flat_count = latents.shape
    half = observe_weight.shape[0] // 9
    lanes = 2 * half
    pairs = flat_count // lanes
    hidden = in_weight.shape[2]
    obs_cols, obs_lanes = obs_cells.shape[1], obs_values.shape[1]
    ens = mem_n * members
    ext = rows + 2 * HALO
    operands = (
        latents, in_weight, out_weight.transpose(0, 2, 1), observe_weight.T, obs_cells, obs_values, obs_precision
    )
    vmem = pl.BlockSpec(memory_space=pltpu.VMEM)
    dma = pltpu.SemaphoreType.DMA
    analysis, covariance = pl.pallas_call(
        functools.partial(kernel, sizes),
        out_shape=(
            jax.ShapeDtypeStruct((members, rows, pairs, lanes), F32),
            jax.ShapeDtypeStruct((ens, ens), F32),
        ),
        in_specs=[pl.BlockSpec(memory_space=pltpu.HBM)] * 7,
        out_specs=(vmem, vmem),
        scratch_shapes=[pltpu.VMEM(x.shape, x.dtype) for x in operands] + [
            dma((7,)),
            pltpu.VMEM((2, members, rows, flat_count), BF16),
            pltpu.VMEM((pairs * rows, lanes), F32),
            pltpu.VMEM((members, ext, pairs, lanes), BF16),
            pltpu.VMEM((members, ext, pairs, 2 * lanes), BF16),
            pltpu.VMEM((members, ext, pairs, 2 * hidden), BF16),
            pltpu.VMEM((members, ext, pairs, lanes), BF16),
            pltpu.VMEM((2, 12 * half, 2 * hidden), BF16),
            pltpu.VMEM((2, 2 * lanes, 6 * hidden), BF16),
            pltpu.VMEM((obs_lanes, 24 * half), BF16),
            pltpu.VMEM((members * rows * obs_cols, 24 * half), BF16),
            pltpu.VMEM((mem_n, members, rows, pairs, lanes), BF16),
            pltpu.VMEM((2, members, pairs, lanes), BF16),
            pltpu.VMEM((mem_n * members * rows, obs_lanes), F32),
            pltpu.VMEM((obs_lanes // 128, ens * rows, 128), F32),
            pltpu.VMEM((tile_n, ens, 128), F32),
            dma((2,)), dma((2,)), dma((2, members)), dma((2, members)),
            dma((mem_n,)), dma((mem_n,)),
            dma((mem_n, members)), dma((mem_n, members)), dma((mem_n, members)),
            dma((tile_n,)), dma((tile_n,)),
        ],
        compiler_params=pltpu.CompilerParams(
            collective_id=0, has_side_effects=True, vmem_limit_bytes=56 * 1024 * 1024
        ),
    )(*operands)
    return analysis.reshape(members, rows, flat_count), covariance


def solution(mesh):
    in_specs = (
        P("mem", "tile", None), P(), P(), P(), P("tile", None), P("tile", None), P("tile", None),
    )
    out_specs = (P("mem", "tile", None), P())
    sizes = (mesh.shape["mem"], mesh.shape["tile"])
    return jax.shard_map(
        functools.partial(per_device, sizes), mesh=mesh, in_specs=in_specs, out_specs=out_specs, check_vma=False
    )
```

```python
import functools

import jax
import jax.numpy as jnp
from jax import lax
from jax.experimental import pallas as pl
from jax.experimental.pallas import tpu as pltpu
from jax.sharding import PartitionSpec as P

EPS = 1e-06
GUIDE_STEP = 0.5
HALO = 4
BF16 = jnp.bfloat16
F32 = jnp.float32
HIGHEST = lax.Precision.HIGHEST


def iota(shape, axis):
    return lax.broadcasted_iota(jnp.int32, shape, axis)


def neighbours(values, pairs, half, swap):
    count, lanes = values.shape
    pair = iota((1, pairs, lanes), 1)
    low = iota((1, pairs, lanes), 2) < half
    following = pltpu.roll(values, count - 1, 0).reshape(count // pairs, pairs, lanes)
    previous = pltpu.roll(values, 1, 0).reshape(count // pairs, pairs, lanes)
    if swap:
        outside = (low & (pair == 0)) | (~low & (pair == pairs - 1))
        picked = jnp.where(low, previous, following)
    else:
        outside = (low & (pair == pairs - 1)) | (~low & (pair == 0))
        picked = jnp.where(low, following, previous)
    return jnp.where(outside, 0.0, picked).reshape(count, lanes)


def kernel(
    sizes, *refs
):
    mem_n, tile_n = sizes
    operands, (out, cov_out), local, load_sem, rest = refs[:7], refs[7:9], refs[9:16], refs[16], refs[17:]
    lat, w_in, w_out, w_obs, cells, values, precision = local
    (
    halo, stage, raw, frame, hid, cur, big_in, big_out, big_obs, patch, gathered, edge, preds, chunks, covs,
    halo_send, halo_recv, edge_send, edge_recv, pred_send, pred_recv,
    bulk_send, fwd_send, bulk_recv, cov_send, cov_recv,
    ) = rest
    members, rows, flat_count = lat.shape
    half = w_obs.shape[1] // 9
    lanes = 2 * half
    pairs = flat_count // lanes
    hidden = w_in.shape[2]
    obs_cols = cells.shape[1]
    obs_lanes = values.shape[1]
    obs_ch = w_obs.shape[0]
    ens = mem_n * members
    me, tile = lax.axis_index("mem"), lax.axis_index("tile")
    ext = rows + 2 * HALO

    def mem_peer(k):
        return lax.rem(me + k, mem_n)

    def tile_peer(k):
        return lax.rem(tile + k, tile_n)

    loads = [
        pltpu.make_async_copy(source, dest, load_sem.at[i])
        for i, (source, dest) in enumerate(zip(operands, local))
    ]
    for load in loads:
        load.start()
    barrier = pltpu.get_barrier_semaphore()
    for k in range(1, mem_n):
        pl.semaphore_signal(barrier, inc=1, device_id={"mem": mem_peer(k)}, device_id_type=pl.DeviceIdType.MESH)
    for k in range(1, tile_n):
        pl.semaphore_signal(barrier, inc=1, device_id={"tile": tile_peer(k)}, device_id_type=pl.DeviceIdType.MESH)
    def remote(src, dst, send, recv, axis, index):
        return pltpu.make_async_remote_copy(
            src_ref=src, dst_ref=dst, send_sem=send, recv_sem=recv,
            device_id={axis: index}, device_id_type=pl.DeviceIdType.MESH,
        )

    to_next = [remote(
        operands[0].at[m], halo.at[0, m], halo_send.at[0, m], halo_recv.at[0, m],
        "tile", jnp.minimum(tile + 1, tile_n - 1),
    ) for m in range(members)]
    to_prev = [remote(
        operands[0].at[m], halo.at[1, m], halo_send.at[1, m], halo_recv.at[1, m],
        "tile", jnp.maximum(tile - 1, 0),
    ) for m in range(members)]
    has_next, has_prev = tile < tile_n - 1, tile > 0

    def build_in(layer):
        zero = jnp.zeros((half, hidden), BF16)
        for di in range(3):
            tap = lambda dj: w_in[layer, pl.ds((di * 3 + dj) * half, half), :] * BF16(0.5)
            blocks = ((tap(1), tap(0)), (tap(2), tap(1)), (zero, tap(2)), (tap(0), zero))
            for b, (even, odd) in enumerate(blocks):
                at = pl.ds((di * 4 + b) * half, half)
                big_in[layer, at, pl.ds(0, hidden)] = even
                big_in[layer, at, pl.ds(hidden, hidden)] = odd

    def build_out(layer):
        zero = jnp.zeros((half, hidden), BF16)
        for di in range(3):
            tap = lambda dj: w_out[layer, :, pl.ds((di * 3 + dj) * hidden, hidden)]
            blocks = ((tap(1), tap(2)), (tap(0), tap(1)), (zero, tap(0)), (tap(2), zero))
            for b, (even, odd) in enumerate(blocks):
                at = pl.ds(b * half, half)
                big_out[layer, at, pl.ds(di * 2 * hidden, hidden)] = even
                big_out[layer, at, pl.ds((di * 2 + 1) * hidden, hidden)] = odd

    def build_obs():
        weight = w_obs[...]
        zero = jnp.zeros((obs_ch, half), BF16)
        blocks = []
        for parity in range(2):
            for di in range(3):
                tap = lambda dj: weight[:, (di * 3 + dj) * half : (di * 3 + dj + 1) * half]
                blocks += [[tap(1), tap(2), zero, tap(0)], [tap(0), tap(1), tap(2), zero]][parity]
        same_ch = (iota((obs_ch, obs_ch), 0) == iota((obs_ch, obs_ch), 1)).astype(F32)
        spread_ch = jnp.concatenate([same_ch] * obs_cols, axis=0)
        big_obs[...] = jnp.dot(
            spread_ch.astype(BF16), jnp.concatenate(blocks, axis=1), preferred_element_type=F32
        ).astype(BF16)

    def unfold(slot, source, m):
        for p in range(pairs):
            tile_p = source[m, :, pl.ds(p * lanes, lanes)] if slot is None else source[slot, m, :, pl.ds(p * lanes, lanes)]
            stage[m, pl.ds(p * rows, rows), :] = tile_p.astype(F32)

    def unfolded(m, first, count):
        return jnp.concatenate(
            [stage[m, pl.ds(first + r, pairs, stride=rows), :] for r in range(count)], axis=0
        )

    def take(slot, source, m, first, start, count):
        unfold(slot, source, m)
        wide = unfolded(m, first, count)
        put(raw, m, start, count, wide.astype(BF16))
        put(frame, m, start, count, norm_frame(wide))

    block = ((iota((lanes, lanes), 0) < half) == (iota((lanes, lanes), 1) < half)).astype(BF16)
    ones = jnp.concatenate([block, block], axis=0)

    def norm_frame(x):
        wide = x.astype(F32)
        square = wide * wide
        high = square.astype(BF16)
        low = (square - high.astype(F32)).astype(BF16)
        total = jnp.dot(jnp.concatenate([high, low], axis=1), ones, preferred_element_type=F32)
        normed = wide * lax.rsqrt(total * (1.0 / half) + EPS)
        return with_sides(normed)

    def with_sides(v):
        return jnp.concatenate([v, neighbours(v, pairs, half, False)], axis=1).astype(BF16)

    def flat(ref, m, start, count):
        return ref[m, pl.ds(start, count)].reshape(count * pairs, ref.shape[-1])

    def put(ref, m, start, count, value):
        ref[m, pl.ds(start, count)] = value.reshape(count, pairs, ref.shape[-1])

    def taps(ref, m, start, count):
        return jnp.concatenate([flat(ref, m, start + d - 1, count) for d in range(3)], axis=1)

    def conv_in(layer, m, start, count):
        summed = jnp.dot(taps(frame, m, start, count), big_in[layer], preferred_element_type=F32)
        act = summed + summed * jnp.tanh(summed)
        put(hid, m, start, count, act.astype(BF16))

    def conv_sum(layer, lhs, before):
        summed = lax.dot_general(
            lhs, big_out[layer], (((1,), (1,)), ((), ())), preferred_element_type=F32
        )
        summed = summed[:, :lanes] + neighbours(summed[:, lanes:], pairs, half, True)
        return (before.astype(F32) + summed).astype(BF16)

    def conv_out(layer, m, start, count, before):
        return conv_sum(layer, taps(hid, m, start, count), before)

    def blank(ref, low, high):
        def clear(start, count):
            ref[:, pl.ds(start, count)] = jnp.zeros((members, count) + ref.shape[2:], BF16)
        pl.when(tile == 0)(lambda: clear(low, HALO - low))
        pl.when(tile == tile_n - 1)(lambda: clear(HALO + rows, high - HALO - rows))

    def each_member(body):
        for m in range(members):
            body(m)

    pl.semaphore_wait(barrier, mem_n - 1 + tile_n - 1)
    for m in range(members):
        pl.when(has_next)(lambda: to_next[m].start())
        pl.when(has_prev)(lambda: to_prev[m].start())
    loads[0].wait()
    each_member(lambda m: take(None, lat, m, 0, HALO, rows))
    loads[1].wait()
    build_in(0)
    each_member(lambda m: conv_in(0, m, HALO + 1, rows - 2))
    for load in loads[2:]:
        load.wait()
    build_out(0)
    build_in(1)
    build_out(1)
    build_obs()
    eye = (iota((obs_cols, obs_cols), 0) == iota((obs_cols, obs_cols), 1)).astype(BF16)
    cells_t = lax.dot_general(
        eye, cells[...].astype(F32).astype(BF16), (((1,), (1,)), ((), ())), preferred_element_type=F32
    ).astype(jnp.int32)

    @pl.when(tile == 0)
    def _():
        halo[0] = jnp.zeros(halo.shape[1:], BF16)

    @pl.when(tile == tile_n - 1)
    def _():
        halo[1] = jnp.zeros(halo.shape[1:], BF16)

    def outer_rows(m):
        pl.when(has_prev)(lambda: to_next[m].wait_recv())
        pl.when(has_next)(lambda: to_prev[m].wait_recv())
        take(0, halo, m, rows - HALO, 0, HALO)
        take(1, halo, m, 0, HALO + rows, HALO)
        conv_in(0, m, 1, HALO)
        conv_in(0, m, HALO + rows - 1, HALO)

    def first_out(m):
        put(cur, m, 2, ext - 4, conv_out(0, m, 2, ext - 4, flat(raw, m, 2, ext - 4)))

    def second_in(m):
        put(frame, m, 2, ext - 4, norm_frame(flat(cur, m, 2, ext - 4)))
        conv_in(1, m, 3, ext - 6)

    each_member(outer_rows)
    blank(hid, 1, ext - 1)
    each_member(first_out)
    blank(cur, 2, ext - 2)
    each_member(second_in)
    blank(hid, 3, ext - 3)

    step = 2 if mem_n % 2 == 0 else 1
    sibling = me + 1 - 2 * lax.rem(me, 2)
    edge_next, edge_prev, bulk, forwards = [], [], [], []

    def share(m):
        block = gathered.at[me, m]
        for k in range(step, mem_n, step):
            bulk.append(remote(block, block, bulk_send.at[k, m], bulk_recv.at[me, m], "mem", mem_peer(k)))
        if step == 2:
            bulk.append(remote(block, block, bulk_send.at[0, m], bulk_recv.at[me, m], "mem", sibling))
        for copy in bulk[-(mem_n // step if step == 2 else mem_n - 1):]:
            copy.start()

    def arrived(k, m):
        j = mem_peer(k)
        block = gathered.at[j, m]
        remote(block, block, bulk_send.at[0, m], bulk_recv.at[j, m], "mem", j).wait_recv()

    def pass_on(m):
        if step == 2:
            for k in range(2, mem_n, 2):
                arrived(k, m)
                j = mem_peer(k)
                block = gathered.at[j, m]
                copy = remote(block, block, fwd_send.at[k, m], bulk_recv.at[j, m], "mem", sibling)
                copy.start()
                forwards.append(copy)

    early = (members + 1) // 2

    def finish(picked):
        lhs = jnp.concatenate([taps(hid, m, HALO + r, count) for m, r, count in picked], axis=0)
        before = jnp.concatenate([flat(cur, m, HALO + r, count) for m, r, count in picked], axis=0)
        done = conv_sum(1, lhs, before)
        sides = with_sides(done.astype(F32))
        at = 0
        for m, r, count in picked:
            end = at + count * pairs
            gathered[me, m, pl.ds(r, count)] = done[at:end].reshape(count, pairs, lanes)
            put(frame, m, HALO + r, count, sides[at:end])
            at = end

    finish([(m, r, 1) for m in range(members) for r in sorted({0, rows - 1})])
    for m in range(members):
        edge_next.append(remote(
            gathered.at[me, m, rows - 1], edge.at[0, m], edge_send.at[0, m], edge_recv.at[0, m],
            "tile", jnp.minimum(tile + 1, tile_n - 1),
        ))
        edge_prev.append(remote(
            gathered.at[me, m, 0], edge.at[1, m], edge_send.at[1, m], edge_recv.at[1, m],
            "tile", jnp.maximum(tile - 1, 0),
        ))
        pl.when(has_next)(lambda: edge_next[m].start())
        pl.when(has_prev)(lambda: edge_prev[m].start())
    finish([(m, 1, rows - 2) for m in range(members)])
    for m in range(early):
        share(m)

    column = 2 * iota((obs_cols, pairs), 1)
    wide = 12 * half

    first_lane = iota((1, obs_cols, obs_lanes), 1) * obs_ch
    lane = iota((1, obs_cols, obs_lanes), 2)
    own = (lane >= first_lane) & (lane < first_lane + obs_ch)
    per = members * rows

    def observe(base, chosen):
        for i, r in enumerate(chosen):
            here = cells_t[:, r : r + 1]
            pick = jnp.concatenate([(here == column), (here == column + 1)], axis=0).astype(BF16)
            around = jnp.concatenate([taps(frame, m, HALO + r, 1) for m in range(members)], axis=1)
            got = jnp.dot(pick, around, preferred_element_type=F32).astype(BF16)
            for m in range(members):
                part = got[:, m * wide : (m + 1) * wide]
                at = pl.ds((base + i * members + m) * obs_cols, obs_cols)
                patch[at, pl.ds(0, wide)] = part[:obs_cols]
                patch[at, pl.ds(wide, wide)] = part[obs_cols:]
        count = len(chosen) * members
        spread_pred = lax.dot_general(
            patch[pl.ds(base * obs_cols, count * obs_cols), :], big_obs[...], (((1,), (1,)), ((), ())),
            preferred_element_type=F32,
        ).reshape(count, obs_cols, obs_lanes)
        found = jnp.sum(jnp.where(own, spread_pred, 0.0), axis=1)
        for i, r in enumerate(chosen):
            for m in range(members):
                preds[pl.ds(me * per + m * rows + r, 1), :] = found[i * members + m : i * members + m + 1]

    inner, outer = list(range(1, rows - 1)), sorted({0, rows - 1})
    observe(0, inner)
    for m in range(members):
        pl.when(has_prev)(lambda: edge_next[m].wait_recv())
        pl.when(has_next)(lambda: edge_prev[m].wait_recv())

    @pl.when(tile == 0)
    def _():
        edge[0] = jnp.zeros(edge.shape[1:], BF16)

    @pl.when(tile == tile_n - 1)
    def _():
        edge[1] = jnp.zeros(edge.shape[1:], BF16)

    for m in range(members):
        frame[m, HALO - 1] = with_sides(edge[0, m].astype(F32))
        frame[m, HALO + rows] = with_sides(edge[1, m].astype(F32))
    observe(len(inner) * members, outer)
    mine_at = pl.ds(pl.multiple_of(me * per, per), per)
    pred_copies = [
        remote(preds.at[mine_at], preds.at[mine_at], pred_send.at[k], pred_recv.at[me], "mem", mem_peer(k))
        for k in range(1, mem_n)
    ]
    for copy in pred_copies:
        copy.start()
    for m in range(early, members):
        share(m)
    for k in range(1, mem_n):
        j = mem_peer(k)
        block = preds.at[pl.ds(pl.multiple_of(j * per, per), per)]
        remote(block, block, pred_send.at[k], pred_recv.at[j], "mem", j).wait_recv()

    left, right = [], []
    for c in range(0, obs_lanes, 128):
        chunks[c // 128] = preds[:, pl.ds(c, 128)]
    for r in range(rows):
        for c in range(0, obs_lanes, 128):
            at = pl.ds(c, 128)
            here = chunks[c // 128, pl.ds(r, ens, stride=rows), :]
            mean = jnp.sum(here, axis=0, keepdims=True) * (1.0 / ens)
            left.append((here - mean) * precision[pl.ds(r, 1), at])
            right.append(values[pl.ds(r, 1), at] - here)
    part = lax.dot_general(
        jnp.concatenate(left, axis=1), jnp.concatenate(right, axis=1), (((1,), (1,)), ((), ())),
        precision=HIGHEST, preferred_element_type=F32,
    )
    covs[tile] = jnp.concatenate([part, jnp.zeros((ens, covs.shape[2] - ens), F32)], axis=1)
    cov_copies = [
        remote(covs.at[tile], covs.at[tile], cov_send.at[k], cov_recv.at[tile], "tile", tile_peer(k))
        for k in range(1, tile_n)
    ]
    for copy in cov_copies:
        copy.start()

    for m in range(members):
        pass_on(m)
    for k in range(1, tile_n):
        j = tile_peer(k)
        remote(covs.at[j], covs.at[j], cov_send.at[k], cov_recv.at[j], "tile", j).wait_recv()
    cov = covs[0]
    for j in range(1, tile_n):
        cov = cov + covs[j]
    cov = cov[:, :ens] * (1.0 / (rows * tile_n * obs_lanes))
    cov_out[...] = cov
    centred = GUIDE_STEP * (cov - jnp.mean(cov, axis=0, keepdims=True))
    factors = []
    for q in range(members):
        mine = iota((ens, ens), 1) == me * members + q
        column_q = jnp.sum(jnp.where(mine, centred, 0.0), axis=1, keepdims=True)
        factors.append(jnp.broadcast_to(column_q, (ens, lanes)))

    for k in range(1, mem_n, step):
        for m in range(members):
            arrived(k, m)
    for r in range(rows):
        acc = [gathered[me, q, r].astype(F32) for q in range(members)]
        for j in range(ens):
            value = gathered[j // members, j % members, r].astype(F32)
            for q in range(members):
                acc[q] = acc[q] + factors[q][j : j + 1] * value
        for q in range(members):
            stage[q, pl.ds(r, pairs, stride=rows), :] = acc[q]
    for q in range(members):
        for p in range(pairs):
            out[q, :, pl.ds(p * lanes, lanes)] = stage[q, pl.ds(p * rows, rows), :]

    for m in range(members):
        pl.when(has_next)(lambda: to_next[m].wait_send())
        pl.when(has_prev)(lambda: to_prev[m].wait_send())
        pl.when(has_next)(lambda: edge_next[m].wait_send())
        pl.when(has_prev)(lambda: edge_prev[m].wait_send())
    for copy in bulk + pred_copies + cov_copies + forwards:
        copy.wait_send()


def per_device(sizes, latents, in_weight, out_weight, observe_weight, obs_cells, obs_values, obs_precision):
    mem_n, tile_n = sizes
    members, rows, flat_count = latents.shape
    half = observe_weight.shape[0] // 9
    lanes = 2 * half
    pairs = flat_count // lanes
    hidden = in_weight.shape[2]
    obs_cols, obs_lanes = obs_cells.shape[1], obs_values.shape[1]
    ens = mem_n * members
    ext = rows + 2 * HALO
    operands = (
        latents, in_weight, out_weight.transpose(0, 2, 1), observe_weight.T, obs_cells, obs_values, obs_precision
    )
    vmem = pl.BlockSpec(memory_space=pltpu.VMEM)
    dma = pltpu.SemaphoreType.DMA
    analysis, covariance = pl.pallas_call(
        functools.partial(kernel, sizes),
        out_shape=(
            jax.ShapeDtypeStruct((members, rows, flat_count), F32),
            jax.ShapeDtypeStruct((ens, ens), F32),
        ),
        in_specs=[pl.BlockSpec(memory_space=pltpu.HBM)] * 7,
        out_specs=(vmem, vmem),
        scratch_shapes=[pltpu.VMEM(x.shape, x.dtype) for x in operands] + [
            dma((7,)),
            pltpu.VMEM((2, members, rows, flat_count), BF16),
            pltpu.VMEM((members, pairs * rows, lanes), F32),
            pltpu.VMEM((members, ext, pairs, lanes), BF16),
            pltpu.VMEM((members, ext, pairs, 2 * lanes), BF16),
            pltpu.VMEM((members, ext, pairs, 2 * hidden), BF16),
            pltpu.VMEM((members, ext, pairs, lanes), BF16),
            pltpu.VMEM((2, 12 * half, 2 * hidden), BF16),
            pltpu.VMEM((2, 2 * lanes, 6 * hidden), BF16),
            pltpu.VMEM((obs_lanes, 24 * half), BF16),
            pltpu.VMEM((members * rows * obs_cols, 24 * half), BF16),
            pltpu.VMEM((mem_n, members, rows, pairs, lanes), BF16),
            pltpu.VMEM((2, members, pairs, lanes), BF16),
            pltpu.VMEM((mem_n * members * rows, obs_lanes), F32),
            pltpu.VMEM((obs_lanes // 128, ens * rows, 128), F32),
            pltpu.VMEM((tile_n, ens, 128), F32),
            dma((2, members)), dma((2, members)), dma((2, members)), dma((2, members)),
            dma((mem_n,)), dma((mem_n,)),
            dma((mem_n, members)), dma((mem_n, members)), dma((mem_n, members)),
            dma((tile_n,)), dma((tile_n,)),
        ],
        compiler_params=pltpu.CompilerParams(
            collective_id=0, has_side_effects=True, vmem_limit_bytes=56 * 1024 * 1024
        ),
    )(*operands)
    return analysis, covariance


def solution(mesh):
    in_specs = (
        P("mem", "tile", None), P(), P(), P(), P("tile", None), P("tile", None), P("tile", None),
    )
    out_specs = (P("mem", "tile", None), P())
    sizes = (mesh.shape["mem"], mesh.shape["tile"])
    return jax.shard_map(
        functools.partial(per_device, sizes), mesh=mesh, in_specs=in_specs, out_specs=out_specs, check_vma=False
    )
```

```python
import functools

import jax
import jax.numpy as jnp
from jax import lax
from jax.experimental import pallas as pl
from jax.experimental.pallas import tpu as pltpu
from jax.sharding import PartitionSpec as P

EPS = 1e-06
GUIDE_STEP = 0.5
HALO = 4
BF16 = jnp.bfloat16
F32 = jnp.float32
HIGHEST = lax.Precision.HIGHEST


def iota(shape, axis):
    return lax.broadcasted_iota(jnp.int32, shape, axis)


def neighbours(values, pairs, half, swap):
    count, lanes = values.shape
    pair = iota((1, pairs, lanes), 1)
    low = iota((1, pairs, lanes), 2) < half
    following = pltpu.roll(values, count - 1, 0).reshape(count // pairs, pairs, lanes)
    previous = pltpu.roll(values, 1, 0).reshape(count // pairs, pairs, lanes)
    if swap:
        outside = (low & (pair == 0)) | (~low & (pair == pairs - 1))
        picked = jnp.where(low, previous, following)
    else:
        outside = (low & (pair == pairs - 1)) | (~low & (pair == 0))
        picked = jnp.where(low, following, previous)
    return jnp.where(outside, 0.0, picked).reshape(count, lanes)


def kernel(
    sizes, *refs
):
    mem_n, tile_n = sizes
    operands, (gathered, cov_out), local, load_sem, rest = refs[:7], refs[7:9], refs[9:16], refs[16], refs[17:]
    lat, w_in, w_out, w_obs, cells, values, precision = local
    (
    halo, stage, raw, frame, hid, cur, big_in, big_out, big_obs, patch, denoised, edge, preds, chunks, covs,
    halo_send, halo_recv, edge_send, edge_recv, pred_send, pred_recv,
    bulk_send, fwd_send, bulk_recv, cov_send, cov_recv, keep_sem,
    ) = rest
    members, rows, flat_count = lat.shape
    half = w_obs.shape[1] // 9
    lanes = 2 * half
    pairs = flat_count // lanes
    hidden = w_in.shape[2]
    obs_cols = cells.shape[1]
    obs_lanes = values.shape[1]
    obs_ch = w_obs.shape[0]
    ens = mem_n * members
    me, tile = lax.axis_index("mem"), lax.axis_index("tile")
    ext = rows + 2 * HALO

    def mem_peer(k):
        return lax.rem(me + k, mem_n)

    def tile_peer(k):
        return lax.rem(tile + k, tile_n)

    loads = [
        pltpu.make_async_copy(source, dest, load_sem.at[i])
        for i, (source, dest) in enumerate(zip(operands, local))
    ]
    for load in loads:
        load.start()
    barrier = pltpu.get_barrier_semaphore()
    for k in range(1, mem_n):
        pl.semaphore_signal(barrier, inc=1, device_id={"mem": mem_peer(k)}, device_id_type=pl.DeviceIdType.MESH)
    for k in range(1, tile_n):
        pl.semaphore_signal(barrier, inc=1, device_id={"tile": tile_peer(k)}, device_id_type=pl.DeviceIdType.MESH)
    def remote(src, dst, send, recv, axis, index):
        return pltpu.make_async_remote_copy(
            src_ref=src, dst_ref=dst, send_sem=send, recv_sem=recv,
            device_id={axis: index}, device_id_type=pl.DeviceIdType.MESH,
        )

    to_next = [remote(
        operands[0].at[m], halo.at[0, m], halo_send.at[0, m], halo_recv.at[0, m],
        "tile", jnp.minimum(tile + 1, tile_n - 1),
    ) for m in range(members)]
    to_prev = [remote(
        operands[0].at[m], halo.at[1, m], halo_send.at[1, m], halo_recv.at[1, m],
        "tile", jnp.maximum(tile - 1, 0),
    ) for m in range(members)]
    has_next, has_prev = tile < tile_n - 1, tile > 0

    def build_in(layer):
        zero = jnp.zeros((half, hidden), BF16)
        for di in range(3):
            tap = lambda dj: w_in[layer, pl.ds((di * 3 + dj) * half, half), :] * BF16(0.5)
            blocks = ((tap(1), tap(0)), (tap(2), tap(1)), (zero, tap(2)), (tap(0), zero))
            for b, (even, odd) in enumerate(blocks):
                at = pl.ds((di * 4 + b) * half, half)
                big_in[layer, at, pl.ds(0, hidden)] = even
                big_in[layer, at, pl.ds(hidden, hidden)] = odd

    def build_out(layer):
        zero = jnp.zeros((half, hidden), BF16)
        for di in range(3):
            tap = lambda dj: w_out[layer, :, pl.ds((di * 3 + dj) * hidden, hidden)]
            blocks = ((tap(1), tap(2)), (tap(0), tap(1)), (zero, tap(0)), (tap(2), zero))
            for b, (even, odd) in enumerate(blocks):
                at = pl.ds(b * half, half)
                big_out[layer, at, pl.ds(di * 2 * hidden, hidden)] = even
                big_out[layer, at, pl.ds((di * 2 + 1) * hidden, hidden)] = odd

    def build_obs():
        weight = w_obs[...]
        zero = jnp.zeros((obs_ch, half), BF16)
        blocks = []
        for parity in range(2):
            for di in range(3):
                tap = lambda dj: weight[:, (di * 3 + dj) * half : (di * 3 + dj + 1) * half]
                blocks += [[tap(1), tap(2), zero, tap(0)], [tap(0), tap(1), tap(2), zero]][parity]
        same_ch = (iota((obs_ch, obs_ch), 0) == iota((obs_ch, obs_ch), 1)).astype(F32)
        spread_ch = jnp.concatenate([same_ch] * obs_cols, axis=0)
        big_obs[...] = jnp.dot(
            spread_ch.astype(BF16), jnp.concatenate(blocks, axis=1), preferred_element_type=F32
        ).astype(BF16)

    def unfold(slot, source, m):
        for p in range(pairs):
            tile_p = source[m, :, pl.ds(p * lanes, lanes)] if slot is None else source[slot, m, :, pl.ds(p * lanes, lanes)]
            stage[m, pl.ds(p * rows, rows), :] = tile_p.astype(F32)

    def unfolded(m, first, count):
        return jnp.concatenate(
            [stage[m, pl.ds(first + r, pairs, stride=rows), :] for r in range(count)], axis=0
        )

    def take(slot, source, m, first, start, count):
        unfold(slot, source, m)
        wide = unfolded(m, first, count)
        put(raw, m, start, count, wide.astype(BF16))
        put(frame, m, start, count, norm_frame(wide))

    block = ((iota((lanes, lanes), 0) < half) == (iota((lanes, lanes), 1) < half)).astype(BF16)
    ones = jnp.concatenate([block, block], axis=0)

    def norm_frame(x):
        wide = x.astype(F32)
        square = wide * wide
        high = square.astype(BF16)
        low = (square - high.astype(F32)).astype(BF16)
        total = jnp.dot(jnp.concatenate([high, low], axis=1), ones, preferred_element_type=F32)
        normed = wide * lax.rsqrt(total * (1.0 / half) + EPS)
        return with_sides(normed)

    def with_sides(v):
        return jnp.concatenate([v, neighbours(v, pairs, half, False)], axis=1).astype(BF16)

    def flat(ref, m, start, count):
        return ref[m, pl.ds(start, count)].reshape(count * pairs, ref.shape[-1])

    def put(ref, m, start, count, value):
        ref[m, pl.ds(start, count)] = value.reshape(count, pairs, ref.shape[-1])

    def taps(ref, m, start, count):
        return jnp.concatenate([flat(ref, m, start + d - 1, count) for d in range(3)], axis=1)

    def conv_in(layer, m, start, count):
        summed = jnp.dot(taps(frame, m, start, count), big_in[layer], preferred_element_type=F32)
        act = summed + summed * jnp.tanh(summed)
        put(hid, m, start, count, act.astype(BF16))

    def conv_sum(layer, lhs, before):
        summed = lax.dot_general(
            lhs, big_out[layer], (((1,), (1,)), ((), ())), preferred_element_type=F32
        )
        summed = summed[:, :lanes] + neighbours(summed[:, lanes:], pairs, half, True)
        return (before.astype(F32) + summed).astype(BF16)

    def conv_out(layer, m, start, count, before):
        return conv_sum(layer, taps(hid, m, start, count), before)

    def blank(ref, low, high):
        def clear(start, count):
            ref[:, pl.ds(start, count)] = jnp.zeros((members, count) + ref.shape[2:], BF16)
        pl.when(tile == 0)(lambda: clear(low, HALO - low))
        pl.when(tile == tile_n - 1)(lambda: clear(HALO + rows, high - HALO - rows))

    def each_member(body):
        for m in range(members):
            body(m)

    pl.semaphore_wait(barrier, mem_n - 1 + tile_n - 1)
    for m in range(members):
        pl.when(has_next)(lambda: to_next[m].start())
        pl.when(has_prev)(lambda: to_prev[m].start())
    loads[0].wait()
    each_member(lambda m: take(None, lat, m, 0, HALO, rows))
    loads[1].wait()
    build_in(0)
    each_member(lambda m: conv_in(0, m, HALO + 1, rows - 2))
    for load in loads[2:]:
        load.wait()
    build_out(0)
    build_in(1)
    build_out(1)
    build_obs()
    eye = (iota((obs_cols, obs_cols), 0) == iota((obs_cols, obs_cols), 1)).astype(BF16)
    cells_t = lax.dot_general(
        eye, cells[...].astype(F32).astype(BF16), (((1,), (1,)), ((), ())), preferred_element_type=F32
    ).astype(jnp.int32)

    @pl.when(tile == 0)
    def _():
        halo[0] = jnp.zeros(halo.shape[1:], BF16)

    @pl.when(tile == tile_n - 1)
    def _():
        halo[1] = jnp.zeros(halo.shape[1:], BF16)

    def outer_rows(m):
        pl.when(has_prev)(lambda: to_next[m].wait_recv())
        pl.when(has_next)(lambda: to_prev[m].wait_recv())
        take(0, halo, m, rows - HALO, 0, HALO)
        take(1, halo, m, 0, HALO + rows, HALO)
        conv_in(0, m, 1, HALO)
        conv_in(0, m, HALO + rows - 1, HALO)

    def first_out(m):
        put(cur, m, 2, ext - 4, conv_out(0, m, 2, ext - 4, flat(raw, m, 2, ext - 4)))

    def second_in(m):
        put(frame, m, 2, ext - 4, norm_frame(flat(cur, m, 2, ext - 4)))
        conv_in(1, m, 3, ext - 6)

    each_member(outer_rows)
    blank(hid, 1, ext - 1)
    each_member(first_out)
    blank(cur, 2, ext - 2)
    each_member(second_in)
    blank(hid, 3, ext - 3)

    step = 2 if mem_n % 2 == 0 else 1
    sibling = me + 1 - 2 * lax.rem(me, 2)
    edge_next, edge_prev, bulk, forwards = [], [], [], []

    def share(m):
        block, place = denoised.at[m], gathered.at[me, m]
        for k in range(step, mem_n, step):
            bulk.append(remote(block, place, bulk_send.at[k, m], bulk_recv.at[me, m], "mem", mem_peer(k)))
        if step == 2:
            bulk.append(remote(block, place, bulk_send.at[0, m], bulk_recv.at[me, m], "mem", sibling))
        for copy in bulk[-(mem_n // step if step == 2 else mem_n - 1):]:
            copy.start()

    def arrived(k, m):
        j = mem_peer(k)
        block = gathered.at[j, m]
        remote(block, block, bulk_send.at[0, m], bulk_recv.at[j, m], "mem", j).wait_recv()

    def pass_on(m):
        if step == 2:
            for k in range(2, mem_n, 2):
                arrived(k, m)
                j = mem_peer(k)
                block = gathered.at[j, m]
                copy = remote(block, block, fwd_send.at[k, m], bulk_recv.at[j, m], "mem", sibling)
                copy.start()
                forwards.append(copy)

    early = (members + 1) // 2

    def finish(picked):
        lhs = jnp.concatenate([taps(hid, m, HALO + r, count) for m, r, count in picked], axis=0)
        before = jnp.concatenate([flat(cur, m, HALO + r, count) for m, r, count in picked], axis=0)
        done = conv_sum(1, lhs, before)
        sides = with_sides(done.astype(F32))
        at = 0
        for m, r, count in picked:
            end = at + count * pairs
            denoised[m, pl.ds(r, count)] = done[at:end].reshape(count, pairs, lanes)
            put(frame, m, HALO + r, count, sides[at:end])
            at = end

    finish([(m, r, 1) for m in range(members) for r in sorted({0, rows - 1})])
    for m in range(members):
        edge_next.append(remote(
            denoised.at[m, rows - 1], edge.at[0, m], edge_send.at[0, m], edge_recv.at[0, m],
            "tile", jnp.minimum(tile + 1, tile_n - 1),
        ))
        edge_prev.append(remote(
            denoised.at[m, 0], edge.at[1, m], edge_send.at[1, m], edge_recv.at[1, m],
            "tile", jnp.maximum(tile - 1, 0),
        ))
        pl.when(has_next)(lambda: edge_next[m].start())
        pl.when(has_prev)(lambda: edge_prev[m].start())
    finish([(m, 1, rows - 2) for m in range(members)])
    for m in range(early):
        share(m)
    keep = pltpu.make_async_copy(denoised, gathered.at[me], keep_sem)
    keep.start()

    column = 2 * iota((obs_cols, pairs), 1)
    wide = 12 * half

    first_lane = iota((1, obs_cols, obs_lanes), 1) * obs_ch
    lane = iota((1, obs_cols, obs_lanes), 2)
    own = (lane >= first_lane) & (lane < first_lane + obs_ch)
    per = members * rows

    def observe(base, chosen):
        for i, r in enumerate(chosen):
            here = cells_t[:, r : r + 1]
            pick = jnp.concatenate([(here == column), (here == column + 1)], axis=0).astype(BF16)
            around = jnp.concatenate([taps(frame, m, HALO + r, 1) for m in range(members)], axis=1)
            got = jnp.dot(pick, around, preferred_element_type=F32).astype(BF16)
            for m in range(members):
                part = got[:, m * wide : (m + 1) * wide]
                at = pl.ds((base + i * members + m) * obs_cols, obs_cols)
                patch[at, pl.ds(0, wide)] = part[:obs_cols]
                patch[at, pl.ds(wide, wide)] = part[obs_cols:]
        count = len(chosen) * members
        spread_pred = lax.dot_general(
            patch[pl.ds(base * obs_cols, count * obs_cols), :], big_obs[...], (((1,), (1,)), ((), ())),
            preferred_element_type=F32,
        ).reshape(count, obs_cols, obs_lanes)
        found = jnp.sum(jnp.where(own, spread_pred, 0.0), axis=1)
        for i, r in enumerate(chosen):
            for m in range(members):
                preds[pl.ds(me * per + m * rows + r, 1), :] = found[i * members + m : i * members + m + 1]

    inner, outer = list(range(1, rows - 1)), sorted({0, rows - 1})
    observe(0, inner)
    for m in range(members):
        pl.when(has_prev)(lambda: edge_next[m].wait_recv())
        pl.when(has_next)(lambda: edge_prev[m].wait_recv())

    @pl.when(tile == 0)
    def _():
        edge[0] = jnp.zeros(edge.shape[1:], BF16)

    @pl.when(tile == tile_n - 1)
    def _():
        edge[1] = jnp.zeros(edge.shape[1:], BF16)

    for m in range(members):
        frame[m, HALO - 1] = with_sides(edge[0, m].astype(F32))
        frame[m, HALO + rows] = with_sides(edge[1, m].astype(F32))
    observe(len(inner) * members, outer)
    mine_at = pl.ds(pl.multiple_of(me * per, per), per)
    pred_copies = [
        remote(preds.at[mine_at], preds.at[mine_at], pred_send.at[k], pred_recv.at[me], "mem", mem_peer(k))
        for k in range(1, mem_n)
    ]
    for copy in pred_copies:
        copy.start()
    for m in range(early, members):
        share(m)
    for k in range(1, mem_n):
        j = mem_peer(k)
        block = preds.at[pl.ds(pl.multiple_of(j * per, per), per)]
        remote(block, block, pred_send.at[k], pred_recv.at[j], "mem", j).wait_recv()

    left, right = [], []
    for c in range(0, obs_lanes, 128):
        chunks[c // 128] = preds[:, pl.ds(c, 128)]
    for r in range(rows):
        for c in range(0, obs_lanes, 128):
            at = pl.ds(c, 128)
            here = chunks[c // 128, pl.ds(r, ens, stride=rows), :]
            mean = jnp.sum(here, axis=0, keepdims=True) * (1.0 / ens)
            left.append((here - mean) * precision[pl.ds(r, 1), at])
            right.append(values[pl.ds(r, 1), at] - here)
    part = lax.dot_general(
        jnp.concatenate(left, axis=1), jnp.concatenate(right, axis=1), (((1,), (1,)), ((), ())),
        precision=HIGHEST, preferred_element_type=F32,
    )
    covs[tile] = jnp.concatenate([part, jnp.zeros((ens, covs.shape[2] - ens), F32)], axis=1)
    cov_copies = [
        remote(covs.at[tile], covs.at[tile], cov_send.at[k], cov_recv.at[tile], "tile", tile_peer(k))
        for k in range(1, tile_n)
    ]
    for copy in cov_copies:
        copy.start()

    for m in range(members):
        pass_on(m)
    for k in range(1, tile_n):
        j = tile_peer(k)
        remote(covs.at[j], covs.at[j], cov_send.at[k], cov_recv.at[j], "tile", j).wait_recv()
    cov = covs[0]
    for j in range(1, tile_n):
        cov = cov + covs[j]
    cov = cov[:, :ens] * (1.0 / (rows * tile_n * obs_lanes))
    cov_out[...] = cov
    for k in range(1, mem_n, step):
        for m in range(members):
            arrived(k, m)
    keep.wait()
    for m in range(members):
        pl.when(has_next)(lambda: to_next[m].wait_send())
        pl.when(has_prev)(lambda: to_prev[m].wait_send())
        pl.when(has_next)(lambda: edge_next[m].wait_send())
        pl.when(has_prev)(lambda: edge_prev[m].wait_send())
    for copy in bulk + pred_copies + cov_copies + forwards:
        copy.wait_send()


def update_kernel(gathered, cov_ref, out, cov_out, stage):
    mem_n, members, rows, pairs, lanes = gathered.shape
    ens = mem_n * members
    me = lax.axis_index("mem")
    cov = cov_ref[...]
    cov_out[...] = cov
    centred = GUIDE_STEP * (cov - jnp.mean(cov, axis=0, keepdims=True))
    factors = []
    for q in range(members):
        mine = iota((ens, ens), 1) == me * members + q
        column_q = jnp.sum(jnp.where(mine, centred, 0.0), axis=1, keepdims=True)
        factors.append(jnp.broadcast_to(column_q, (ens, lanes)))
    for r in range(rows):
        acc = [gathered[me, q, r].astype(F32) for q in range(members)]
        for j in range(ens):
            value = gathered[j // members, j % members, r].astype(F32)
            for q in range(members):
                acc[q] = acc[q] + factors[q][j : j + 1] * value
        for q in range(members):
            stage[q, pl.ds(r, pairs, stride=rows), :] = acc[q]
    for q in range(members):
        for p in range(pairs):
            out[q, :, pl.ds(p * lanes, lanes)] = stage[q, pl.ds(p * rows, rows), :]


def per_device(sizes, latents, in_weight, out_weight, observe_weight, obs_cells, obs_values, obs_precision):
    mem_n, tile_n = sizes
    members, rows, flat_count = latents.shape
    half = observe_weight.shape[0] // 9
    lanes = 2 * half
    pairs = flat_count // lanes
    hidden = in_weight.shape[2]
    obs_cols, obs_lanes = obs_cells.shape[1], obs_values.shape[1]
    ens = mem_n * members
    ext = rows + 2 * HALO
    operands = (
        latents, in_weight, out_weight.transpose(0, 2, 1), observe_weight.T, obs_cells, obs_values, obs_precision
    )
    vmem = pl.BlockSpec(memory_space=pltpu.VMEM)
    dma = pltpu.SemaphoreType.DMA
    everyone, covariance = pl.pallas_call(
        functools.partial(kernel, sizes),
        out_shape=(
            jax.ShapeDtypeStruct((mem_n, members, rows, pairs, lanes), BF16),
            jax.ShapeDtypeStruct((ens, ens), F32),
        ),
        in_specs=[pl.BlockSpec(memory_space=pltpu.HBM)] * 7,
        out_specs=(pl.BlockSpec(memory_space=pltpu.HBM), vmem),
        scratch_shapes=[pltpu.VMEM(x.shape, x.dtype) for x in operands] + [
            dma((7,)),
            pltpu.VMEM((2, members, rows, flat_count), BF16),
            pltpu.VMEM((members, pairs * rows, lanes), F32),
            pltpu.VMEM((members, ext, pairs, lanes), BF16),
            pltpu.VMEM((members, ext, pairs, 2 * lanes), BF16),
            pltpu.VMEM((members, ext, pairs, 2 * hidden), BF16),
            pltpu.VMEM((members, ext, pairs, lanes), BF16),
            pltpu.VMEM((2, 12 * half, 2 * hidden), BF16),
            pltpu.VMEM((2, 2 * lanes, 6 * hidden), BF16),
            pltpu.VMEM((obs_lanes, 24 * half), BF16),
            pltpu.VMEM((members * rows * obs_cols, 24 * half), BF16),
            pltpu.VMEM((members, rows, pairs, lanes), BF16),
            pltpu.VMEM((2, members, pairs, lanes), BF16),
            pltpu.VMEM((mem_n * members * rows, obs_lanes), F32),
            pltpu.VMEM((obs_lanes // 128, ens * rows, 128), F32),
            pltpu.VMEM((tile_n, ens, 128), F32),
            dma((2, members)), dma((2, members)), dma((2, members)), dma((2, members)),
            dma((mem_n,)), dma((mem_n,)),
            dma((mem_n, members)), dma((mem_n, members)), dma((mem_n, members)),
            dma((tile_n,)), dma((tile_n,)), dma,
        ],
        compiler_params=pltpu.CompilerParams(
            collective_id=0, has_side_effects=True, vmem_limit_bytes=56 * 1024 * 1024
        ),
    )(*operands)
    count = 2 if pairs % 32 == 0 else 1
    part = pairs // count
    whole = pl.BlockSpec((ens, ens), lambda i: (0, 0))
    return pl.pallas_call(
        update_kernel,
        grid=(count,),
        out_shape=(
            jax.ShapeDtypeStruct((members, rows, flat_count), F32),
            jax.ShapeDtypeStruct((ens, ens), F32),
        ),
        in_specs=[pl.BlockSpec((mem_n, members, rows, part, lanes), lambda i: (0, 0, 0, i, 0)), whole],
        out_specs=(pl.BlockSpec((members, rows, part * lanes), lambda i: (0, 0, i)), whole),
        scratch_shapes=[pltpu.VMEM((members, part * rows, lanes), F32)],
        compiler_params=pltpu.CompilerParams(vmem_limit_bytes=56 * 1024 * 1024),
    )(everyone, covariance)


def solution(mesh):
    in_specs = (
        P("mem", "tile", None), P(), P(), P(), P("tile", None), P("tile", None), P("tile", None),
    )
    out_specs = (P("mem", "tile", None), P())
    sizes = (mesh.shape["mem"], mesh.shape["tile"])
    return jax.shard_map(
        functools.partial(per_device, sizes), mesh=mesh, in_specs=in_specs, out_specs=out_specs, check_vma=False
    )
```

```python
import functools

import jax
import jax.numpy as jnp
from jax import lax
from jax.experimental import pallas as pl
from jax.experimental.pallas import tpu as pltpu
from jax.sharding import PartitionSpec as P

EPS = 1e-06
GUIDE_STEP = 0.5
HALO = 4
BF16 = jnp.bfloat16
F32 = jnp.float32
HIGHEST = lax.Precision.HIGHEST


def iota(shape, axis):
    return lax.broadcasted_iota(jnp.int32, shape, axis)


def neighbours(values, pairs, half, swap):
    count, lanes = values.shape
    pair = iota((1, pairs, lanes), 1)
    low = iota((1, pairs, lanes), 2) < half
    following = pltpu.roll(values, count - 1, 0).reshape(count // pairs, pairs, lanes)
    previous = pltpu.roll(values, 1, 0).reshape(count // pairs, pairs, lanes)
    if swap:
        outside = (low & (pair == 0)) | (~low & (pair == pairs - 1))
        picked = jnp.where(low, previous, following)
    else:
        outside = (low & (pair == pairs - 1)) | (~low & (pair == 0))
        picked = jnp.where(low, following, previous)
    return jnp.where(outside, 0.0, picked).reshape(count, lanes)


def kernel(
    sizes, *refs
):
    mem_n, tile_n = sizes
    operands, (gathered, cov_out), local, load_sem, rest = refs[:7], refs[7:9], refs[9:16], refs[16], refs[17:]
    lat, w_in, w_out, w_obs, cells, values, precision = local
    (
    halo, stage, raw, frame, hid, cur, big_in, big_out, turned, big_obs, patch, denoised, edge, preds, chunks, covs,
    halo_send, halo_recv, edge_send, edge_recv, pred_send, pred_recv,
    bulk_send, fwd_send, bulk_recv, cov_send, cov_recv, keep_sem,
    ) = rest
    members, rows, flat_count = lat.shape
    half = w_obs.shape[1] // 9
    lanes = 2 * half
    pairs = flat_count // lanes
    hidden = w_in.shape[2]
    obs_cols = cells.shape[1]
    obs_lanes = values.shape[1]
    obs_ch = w_obs.shape[0]
    ens = mem_n * members
    me, tile = lax.axis_index("mem"), lax.axis_index("tile")
    ext = rows + 2 * HALO

    def mem_peer(k):
        return lax.rem(me + k, mem_n)

    def tile_peer(k):
        return lax.rem(tile + k, tile_n)

    loads = [
        pltpu.make_async_copy(source, dest, load_sem.at[i])
        for i, (source, dest) in enumerate(zip(operands, local))
    ]
    for load in loads:
        load.start()
    barrier = pltpu.get_barrier_semaphore()
    for k in range(1, mem_n):
        pl.semaphore_signal(barrier, inc=1, device_id={"mem": mem_peer(k)}, device_id_type=pl.DeviceIdType.MESH)
    for k in range(1, tile_n):
        pl.semaphore_signal(barrier, inc=1, device_id={"tile": tile_peer(k)}, device_id_type=pl.DeviceIdType.MESH)
    def remote(src, dst, send, recv, axis, index):
        return pltpu.make_async_remote_copy(
            src_ref=src, dst_ref=dst, send_sem=send, recv_sem=recv,
            device_id={axis: index}, device_id_type=pl.DeviceIdType.MESH,
        )

    to_next = [remote(
        operands[0].at[m], halo.at[0, m], halo_send.at[0, m], halo_recv.at[0, m],
        "tile", jnp.minimum(tile + 1, tile_n - 1),
    ) for m in range(members)]
    to_prev = [remote(
        operands[0].at[m], halo.at[1, m], halo_send.at[1, m], halo_recv.at[1, m],
        "tile", jnp.maximum(tile - 1, 0),
    ) for m in range(members)]
    has_next, has_prev = tile < tile_n - 1, tile > 0

    def build_in(layer):
        zero = jnp.zeros((half, hidden), BF16)
        for di in range(3):
            tap = lambda dj: w_in[layer, pl.ds((di * 3 + dj) * half, half), :] * BF16(0.5)
            blocks = ((tap(1), tap(0)), (tap(2), tap(1)), (zero, tap(2)), (tap(0), zero))
            for b, (even, odd) in enumerate(blocks):
                at = pl.ds((di * 4 + b) * half, half)
                big_in[layer, at, pl.ds(0, hidden)] = even
                big_in[layer, at, pl.ds(hidden, hidden)] = odd

    def build_out(layer):
        zero = jnp.zeros((half, hidden), BF16)
        for di in range(3):
            tap = lambda dj: w_out[layer, :, pl.ds((di * 3 + dj) * hidden, hidden)]
            blocks = ((tap(1), tap(2)), (tap(0), tap(1)), (zero, tap(0)), (tap(2), zero))
            for b, (even, odd) in enumerate(blocks):
                at = pl.ds(b * half, half)
                big_out[layer, at, pl.ds(di * 2 * hidden, hidden)] = even
                big_out[layer, at, pl.ds((di * 2 + 1) * hidden, hidden)] = odd
            at = pl.ds(di * 2 * hidden, 2 * hidden)
            turned[layer, at, :] = big_out[layer, :, at].T

    def build_obs():
        weight = w_obs[...]
        zero = jnp.zeros((obs_ch, half), BF16)
        blocks = []
        for parity in range(2):
            for di in range(3):
                tap = lambda dj: weight[:, (di * 3 + dj) * half : (di * 3 + dj + 1) * half]
                blocks += [[tap(1), tap(2), zero, tap(0)], [tap(0), tap(1), tap(2), zero]][parity]
        same_ch = (iota((obs_ch, obs_ch), 0) == iota((obs_ch, obs_ch), 1)).astype(F32)
        spread_ch = jnp.concatenate([same_ch] * obs_cols, axis=0)
        big_obs[...] = jnp.dot(
            spread_ch.astype(BF16), jnp.concatenate(blocks, axis=1), preferred_element_type=F32
        ).astype(BF16).T

    def unfold(slot, source, m):
        for p in range(pairs):
            tile_p = source[m, :, pl.ds(p * lanes, lanes)] if slot is None else source[slot, m, :, pl.ds(p * lanes, lanes)]
            stage[m, pl.ds(p * rows, rows), :] = tile_p.astype(F32)

    def unfolded(m, first, count):
        return jnp.concatenate(
            [stage[m, pl.ds(first + r, pairs, stride=rows), :] for r in range(count)], axis=0
        )

    def take(slot, source, m, first, start, count):
        unfold(slot, source, m)
        wide = unfolded(m, first, count)
        put(raw, m, start, count, wide.astype(BF16))
        put(frame, m, start, count, norm_frame(wide))

    block = ((iota((lanes, lanes), 0) < half) == (iota((lanes, lanes), 1) < half)).astype(BF16)
    ones = jnp.concatenate([block, block], axis=0)

    def norm_frame(x):
        wide = x.astype(F32)
        square = wide * wide
        high = square.astype(BF16)
        low = (square - high.astype(F32)).astype(BF16)
        total = jnp.dot(jnp.concatenate([high, low], axis=1), ones, preferred_element_type=F32)
        normed = wide * lax.rsqrt(total * (1.0 / half) + EPS)
        return with_sides(normed)

    def with_sides(v):
        return jnp.concatenate([v, neighbours(v, pairs, half, False)], axis=1).astype(BF16)

    def flat(ref, m, start, count):
        return ref[m, pl.ds(start, count)].reshape(count * pairs, ref.shape[-1])

    def put(ref, m, start, count, value):
        ref[m, pl.ds(start, count)] = value.reshape(count, pairs, ref.shape[-1])

    def taps(ref, m, start, count):
        return jnp.concatenate([flat(ref, m, start + d - 1, count) for d in range(3)], axis=1)

    def conv_in(layer, m, start, count):
        summed = jnp.dot(taps(frame, m, start, count), big_in[layer], preferred_element_type=F32)
        act = summed + summed * jnp.tanh(summed)
        put(hid, m, start, count, act.astype(BF16))

    def conv_sum(layer, lhs, before):
        summed = jnp.dot(lhs, turned[layer], preferred_element_type=F32)
        summed = summed[:, :lanes] + neighbours(summed[:, lanes:], pairs, half, True)
        return (before.astype(F32) + summed).astype(BF16)

    def conv_out(layer, m, start, count, before):
        return conv_sum(layer, taps(hid, m, start, count), before)

    def blank(ref, low, high):
        def clear(start, count):
            ref[:, pl.ds(start, count)] = jnp.zeros((members, count) + ref.shape[2:], BF16)
        pl.when(tile == 0)(lambda: clear(low, HALO - low))
        pl.when(tile == tile_n - 1)(lambda: clear(HALO + rows, high - HALO - rows))

    def each_member(body):
        for m in range(members):
            body(m)

    pl.semaphore_wait(barrier, mem_n - 1 + tile_n - 1)
    for m in range(members):
        pl.when(has_next)(lambda: to_next[m].start())
        pl.when(has_prev)(lambda: to_prev[m].start())
    loads[0].wait()
    each_member(lambda m: take(None, lat, m, 0, HALO, rows))
    loads[1].wait()
    build_in(0)
    each_member(lambda m: conv_in(0, m, HALO + 1, rows - 2))
    for load in loads[2:]:
        load.wait()
    build_out(0)
    build_in(1)
    build_out(1)
    build_obs()
    eye = (iota((obs_cols, obs_cols), 0) == iota((obs_cols, obs_cols), 1)).astype(BF16)
    cells_t = lax.dot_general(
        eye, cells[...].astype(F32).astype(BF16), (((1,), (1,)), ((), ())), preferred_element_type=F32
    ).astype(jnp.int32)

    @pl.when(tile == 0)
    def _():
        halo[0] = jnp.zeros(halo.shape[1:], BF16)

    @pl.when(tile == tile_n - 1)
    def _():
        halo[1] = jnp.zeros(halo.shape[1:], BF16)

    def outer_rows(m):
        pl.when(has_prev)(lambda: to_next[m].wait_recv())
        pl.when(has_next)(lambda: to_prev[m].wait_recv())
        take(0, halo, m, rows - HALO, 0, HALO)
        take(1, halo, m, 0, HALO + rows, HALO)
        conv_in(0, m, 1, HALO)
        conv_in(0, m, HALO + rows - 1, HALO)

    def first_out(m):
        put(cur, m, 2, ext - 4, conv_out(0, m, 2, ext - 4, flat(raw, m, 2, ext - 4)))

    def second_in(m):
        put(frame, m, 2, ext - 4, norm_frame(flat(cur, m, 2, ext - 4)))
        conv_in(1, m, 3, ext - 6)

    each_member(outer_rows)
    blank(hid, 1, ext - 1)
    each_member(first_out)
    blank(cur, 2, ext - 2)
    each_member(second_in)
    blank(hid, 3, ext - 3)

    step = 2 if mem_n % 2 == 0 else 1
    sibling = me + 1 - 2 * lax.rem(me, 2)
    edge_next, edge_prev, bulk, forwards = [], [], [], []

    def share(m):
        block, place = denoised.at[m], gathered.at[me, m]
        for k in range(step, mem_n, step):
            bulk.append(remote(block, place, bulk_send.at[k, m], bulk_recv.at[me, m], "mem", mem_peer(k)))
        if step == 2:
            bulk.append(remote(block, place, bulk_send.at[0, m], bulk_recv.at[me, m], "mem", sibling))
        for copy in bulk[-(mem_n // step if step == 2 else mem_n - 1):]:
            copy.start()

    def arrived(k, m):
        j = mem_peer(k)
        block = gathered.at[j, m]
        remote(block, block, bulk_send.at[0, m], bulk_recv.at[j, m], "mem", j).wait_recv()

    def pass_on(m):
        if step == 2:
            for k in range(2, mem_n, 2):
                arrived(k, m)
                j = mem_peer(k)
                block = gathered.at[j, m]
                copy = remote(block, block, fwd_send.at[k, m], bulk_recv.at[j, m], "mem", sibling)
                copy.start()
                forwards.append(copy)

    early = (members + 1) // 2

    def finish(picked):
        lhs = jnp.concatenate([taps(hid, m, HALO + r, count) for m, r, count in picked], axis=0)
        before = jnp.concatenate([flat(cur, m, HALO + r, count) for m, r, count in picked], axis=0)
        done = conv_sum(1, lhs, before)
        sides = with_sides(done.astype(F32))
        at = 0
        for m, r, count in picked:
            end = at + count * pairs
            denoised[m, pl.ds(r, count)] = done[at:end].reshape(count, pairs, lanes)
            put(frame, m, HALO + r, count, sides[at:end])
            at = end

    finish([(m, r, 1) for m in range(members) for r in sorted({0, rows - 1})])
    for m in range(members):
        edge_next.append(remote(
            denoised.at[m, rows - 1], edge.at[0, m], edge_send.at[0, m], edge_recv.at[0, m],
            "tile", jnp.minimum(tile + 1, tile_n - 1),
        ))
        edge_prev.append(remote(
            denoised.at[m, 0], edge.at[1, m], edge_send.at[1, m], edge_recv.at[1, m],
            "tile", jnp.maximum(tile - 1, 0),
        ))
        pl.when(has_next)(lambda: edge_next[m].start())
        pl.when(has_prev)(lambda: edge_prev[m].start())
    finish([(m, 1, rows - 2) for m in range(members)])
    for m in range(early):
        share(m)
    keep = pltpu.make_async_copy(denoised, gathered.at[me], keep_sem)
    keep.start()

    column = 2 * iota((obs_cols, pairs), 1)
    wide = 12 * half

    first_lane = iota((1, obs_cols, obs_lanes), 1) * obs_ch
    lane = iota((1, obs_cols, obs_lanes), 2)
    own = (lane >= first_lane) & (lane < first_lane + obs_ch)
    per = members * rows

    def observe(base, chosen):
        for i, r in enumerate(chosen):
            here = cells_t[:, r : r + 1]
            pick = jnp.concatenate([(here == column), (here == column + 1)], axis=0).astype(BF16)
            around = jnp.concatenate([taps(frame, m, HALO + r, 1) for m in range(members)], axis=1)
            got = jnp.dot(pick, around, preferred_element_type=F32).astype(BF16)
            for m in range(members):
                part = got[:, m * wide : (m + 1) * wide]
                at = pl.ds((base + i * members + m) * obs_cols, obs_cols)
                patch[at, pl.ds(0, wide)] = part[:obs_cols]
                patch[at, pl.ds(wide, wide)] = part[obs_cols:]
        count = len(chosen) * members
        spread_pred = jnp.dot(
            patch[pl.ds(base * obs_cols, count * obs_cols), :], big_obs[...], preferred_element_type=F32
        ).reshape(count, obs_cols, obs_lanes)
        found = jnp.sum(jnp.where(own, spread_pred, 0.0), axis=1)
        for i, r in enumerate(chosen):
            for m in range(members):
                preds[pl.ds(me * per + m * rows + r, 1), :] = found[i * members + m : i * members + m + 1]

    inner, outer = list(range(1, rows - 1)), sorted({0, rows - 1})
    observe(0, inner)
    for m in range(members):
        pl.when(has_prev)(lambda: edge_next[m].wait_recv())
        pl.when(has_next)(lambda: edge_prev[m].wait_recv())

    @pl.when(tile == 0)
    def _():
        edge[0] = jnp.zeros(edge.shape[1:], BF16)

    @pl.when(tile == tile_n - 1)
    def _():
        edge[1] = jnp.zeros(edge.shape[1:], BF16)

    for m in range(members):
        frame[m, HALO - 1] = with_sides(edge[0, m].astype(F32))
        frame[m, HALO + rows] = with_sides(edge[1, m].astype(F32))
    observe(len(inner) * members, outer)
    mine_at = pl.ds(pl.multiple_of(me * per, per), per)
    pred_copies = [
        remote(preds.at[mine_at], preds.at[mine_at], pred_send.at[k], pred_recv.at[me], "mem", mem_peer(k))
        for k in range(1, mem_n)
    ]
    for copy in pred_copies:
        copy.start()
    for m in range(early, members):
        share(m)
    for k in range(1, mem_n):
        j = mem_peer(k)
        block = preds.at[pl.ds(pl.multiple_of(j * per, per), per)]
        remote(block, block, pred_send.at[k], pred_recv.at[j], "mem", j).wait_recv()

    left, right = [], []
    for c in range(0, obs_lanes, 128):
        chunks[c // 128] = preds[:, pl.ds(c, 128)]
    for r in range(rows):
        for c in range(0, obs_lanes, 128):
            at = pl.ds(c, 128)
            here = chunks[c // 128, pl.ds(r, ens, stride=rows), :]
            mean = jnp.sum(here, axis=0, keepdims=True) * (1.0 / ens)
            left.append((here - mean) * precision[pl.ds(r, 1), at])
            right.append(values[pl.ds(r, 1), at] - here)
    part = lax.dot_general(
        jnp.concatenate(left, axis=1), jnp.concatenate(right, axis=1), (((1,), (1,)), ((), ())),
        precision=HIGHEST, preferred_element_type=F32,
    )
    covs[tile] = jnp.concatenate([part, jnp.zeros((ens, covs.shape[2] - ens), F32)], axis=1)
    cov_copies = [
        remote(covs.at[tile], covs.at[tile], cov_send.at[k], cov_recv.at[tile], "tile", tile_peer(k))
        for k in range(1, tile_n)
    ]
    for copy in cov_copies:
        copy.start()

    for m in range(members):
        pass_on(m)
    for k in range(1, tile_n):
        j = tile_peer(k)
        remote(covs.at[j], covs.at[j], cov_send.at[k], cov_recv.at[j], "tile", j).wait_recv()
    cov = covs[0]
    for j in range(1, tile_n):
        cov = cov + covs[j]
    cov = cov[:, :ens] * (1.0 / (rows * tile_n * obs_lanes))
    cov_out[...] = cov
    for k in range(1, mem_n, step):
        for m in range(members):
            arrived(k, m)
    keep.wait()
    for m in range(members):
        pl.when(has_next)(lambda: to_next[m].wait_send())
        pl.when(has_prev)(lambda: to_prev[m].wait_send())
        pl.when(has_next)(lambda: edge_next[m].wait_send())
        pl.when(has_prev)(lambda: edge_prev[m].wait_send())
    for copy in bulk + pred_copies + cov_copies + forwards:
        copy.wait_send()


def update_kernel(gathered, cov_ref, out, cov_out, stage):
    mem_n, members, rows, pairs, lanes = gathered.shape
    ens = mem_n * members
    me = lax.axis_index("mem")
    cov = cov_ref[...]
    cov_out[...] = cov
    centred = GUIDE_STEP * (cov - jnp.mean(cov, axis=0, keepdims=True))
    factors = []
    for q in range(members):
        mine = iota((ens, ens), 1) == me * members + q
        column_q = jnp.sum(jnp.where(mine, centred, 0.0), axis=1, keepdims=True)
        factors.append(jnp.broadcast_to(column_q, (ens, lanes)))
    for r in range(rows):
        acc = [gathered[me, q, r].astype(F32) for q in range(members)]
        for j in range(ens):
            value = gathered[j // members, j % members, r].astype(F32)
            for q in range(members):
                acc[q] = acc[q] + factors[q][j : j + 1] * value
        for q in range(members):
            stage[q, pl.ds(r, pairs, stride=rows), :] = acc[q]
    for q in range(members):
        for p in range(pairs):
            out[q, :, pl.ds(p * lanes, lanes)] = stage[q, pl.ds(p * rows, rows), :]


def per_device(sizes, latents, in_weight, out_weight, observe_weight, obs_cells, obs_values, obs_precision):
    mem_n, tile_n = sizes
    members, rows, flat_count = latents.shape
    half = observe_weight.shape[0] // 9
    lanes = 2 * half
    pairs = flat_count // lanes
    hidden = in_weight.shape[2]
    obs_cols, obs_lanes = obs_cells.shape[1], obs_values.shape[1]
    ens = mem_n * members
    ext = rows + 2 * HALO
    operands = (
        latents, in_weight, out_weight.transpose(0, 2, 1), observe_weight.T, obs_cells, obs_values, obs_precision
    )
    vmem = pl.BlockSpec(memory_space=pltpu.VMEM)
    dma = pltpu.SemaphoreType.DMA
    everyone, covariance = pl.pallas_call(
        functools.partial(kernel, sizes),
        out_shape=(
            jax.ShapeDtypeStruct((mem_n, members, rows, pairs, lanes), BF16),
            jax.ShapeDtypeStruct((ens, ens), F32),
        ),
        in_specs=[pl.BlockSpec(memory_space=pltpu.HBM)] * 7,
        out_specs=(pl.BlockSpec(memory_space=pltpu.HBM), vmem),
        scratch_shapes=[pltpu.VMEM(x.shape, x.dtype) for x in operands] + [
            dma((7,)),
            pltpu.VMEM((2, members, rows, flat_count), BF16),
            pltpu.VMEM((members, pairs * rows, lanes), F32),
            pltpu.VMEM((members, ext, pairs, lanes), BF16),
            pltpu.VMEM((members, ext, pairs, 2 * lanes), BF16),
            pltpu.VMEM((members, ext, pairs, 2 * hidden), BF16),
            pltpu.VMEM((members, ext, pairs, lanes), BF16),
            pltpu.VMEM((2, 12 * half, 2 * hidden), BF16),
            pltpu.VMEM((2, 2 * lanes, 6 * hidden), BF16),
            pltpu.VMEM((2, 6 * hidden, 2 * lanes), BF16),
            pltpu.VMEM((24 * half, obs_lanes), BF16),
            pltpu.VMEM((members * rows * obs_cols, 24 * half), BF16),
            pltpu.VMEM((members, rows, pairs, lanes), BF16),
            pltpu.VMEM((2, members, pairs, lanes), BF16),
            pltpu.VMEM((mem_n * members * rows, obs_lanes), F32),
            pltpu.VMEM((obs_lanes // 128, ens * rows, 128), F32),
            pltpu.VMEM((tile_n, ens, 128), F32),
            dma((2, members)), dma((2, members)), dma((2, members)), dma((2, members)),
            dma((mem_n,)), dma((mem_n,)),
            dma((mem_n, members)), dma((mem_n, members)), dma((mem_n, members)),
            dma((tile_n,)), dma((tile_n,)), dma,
        ],
        compiler_params=pltpu.CompilerParams(
            collective_id=0, has_side_effects=True, vmem_limit_bytes=56 * 1024 * 1024
        ),
    )(*operands)
    count = 2 if pairs % 32 == 0 else 1
    part = pairs // count
    whole = pl.BlockSpec((ens, ens), lambda i: (0, 0))
    return pl.pallas_call(
        update_kernel,
        grid=(count,),
        out_shape=(
            jax.ShapeDtypeStruct((members, rows, flat_count), F32),
            jax.ShapeDtypeStruct((ens, ens), F32),
        ),
        in_specs=[pl.BlockSpec((mem_n, members, rows, part, lanes), lambda i: (0, 0, 0, i, 0)), whole],
        out_specs=(pl.BlockSpec((members, rows, part * lanes), lambda i: (0, 0, i)), whole),
        scratch_shapes=[pltpu.VMEM((members, part * rows, lanes), F32)],
        compiler_params=pltpu.CompilerParams(vmem_limit_bytes=56 * 1024 * 1024),
    )(everyone, covariance)


def solution(mesh):
    in_specs = (
        P("mem", "tile", None), P(), P(), P(), P("tile", None), P("tile", None), P("tile", None),
    )
    out_specs = (P("mem", "tile", None), P())
    sizes = (mesh.shape["mem"], mesh.shape["tile"])
    return jax.shard_map(
        functools.partial(per_device, sizes), mesh=mesh, in_specs=in_specs, out_specs=out_specs, check_vma=False
    )
```
